32 devices in a mesh: dp: 4 (over x, core), fsdp: 8 (over z, y).
Axes of the slice: x: 2, y: 2, z: 4, core: 2. Of those that a mesh axis runs over, the one named last changes fastest.
Arguments:
- gradients: bfloat16 [4, 3072, 2048], P('dp', 'fsdp'), may hold values from -6 to 6
- master: float32 [3072, 2048], P('fsdp', 'dp'), may hold values from -1.3 to 1.3
- moment_one: float32 [3072, 2048], P('fsdp', 'dp'), may hold values from -4 to 4
- moment_two: float32 [3072, 2048], P('fsdp', 'dp'), may hold values from 0.01 to 0.1
- synced: bfloat16 [3072, 2048], P('fsdp', 'dp'), may hold values from -0.75 to 0.75
- rollout: bfloat16 [3072, 2048], P('fsdp', 'dp'), may hold values from -0.77 to 0.77
- amax_record: float32 [24, 16], P('fsdp', 'dp'), may hold values from 0.04 to 1.5
- row_table: int32 [128], replicated, may hold values from 0 to 7, as said below
- expert_owner: int32 [1], replicated, may hold values from 0 to 7
Outputs:
- new_master: float32 [3072, 2048], P('fsdp', 'dp')
- new_one: float32 [3072, 2048], P('fsdp', 'dp')
- new_two: float32 [3072, 2048], P('fsdp', 'dp')
- new_amax: float32 [24, 16], P('fsdp', 'dp')
- new_rollout: bfloat16 [3072, 2048], P('fsdp', 'dp')
The draws below stay inside these ranges and needn't reach their ends.
Inputs may be any that keep to these rules, and one draw needn't show every extreme that they name: `row_table`: each of 0..7 appears exactly 16 times.
All inputs are finite; a program needn't handle non-finite values.
Results may differ from the reference program's by a relative error of at most 0.014.
Values may be sent and summed in bfloat16 or wider, within the bound.
A program may use at most 64 MiB of HBM per device.

```python
import math
import jax
import jax.numpy as jnp
from jax import lax

D = 7168
F = 2048
TILE = 128
ROWS_OWN = 16
WROWS = 3072
EXP_WIN = 1
N_DP = 4
N_FSDP = 8


def base_weights(key):
    key = jax.random.fold_in(key, 17)
    return 0.25 * jnp.clip(jax.random.normal(key, (WROWS, F), jnp.float32), -3.0, 3.0)


def drift_scales(key):
    key = jax.random.fold_in(key, 19)
    return jnp.exp(jax.random.uniform(key, (WROWS // TILE, F // TILE), jnp.float32, math.log(0.1), math.log(0.5)))


def row_classes(key):
    key = jax.random.fold_in(key, 11)
    return (jax.random.permutation(key, TILE) // ROWS_OWN).astype(jnp.int32)


def owner_shifts(key):
    key = jax.random.fold_in(key, 13)
    key_values, key_top, key_low = jax.random.split(key, 3)
    values = jax.random.randint(key_values, (EXP_WIN,), 0, N_FSDP).astype(jnp.int32)
    positions = jnp.arange(EXP_WIN, dtype=jnp.int32)
    top_slot = jax.random.randint(key_top, (), 0, EXP_WIN).astype(jnp.int32)
    values = jnp.where(positions == top_slot, N_FSDP - 1, values)
    if EXP_WIN > 1:
        low_slot = (top_slot + 1 + jax.random.randint(key_low, (), 0, EXP_WIN - 1).astype(jnp.int32)) % EXP_WIN
        values = jnp.where(positions == low_slot, 0, values)
    return values.astype(jnp.int32)


def rollout_order(values, classes, owners):
    block_count = WROWS // TILE
    ordering = jnp.argsort(classes, stable=True).astype(jnp.int32)
    blocks = jnp.arange(block_count, dtype=jnp.int32)
    shifts = owners[blocks * TILE // D]
    first_slot = (jnp.arange(N_FSDP, dtype=jnp.int32)[None, :] - shifts[:, None]) % N_FSDP * ROWS_OWN
    chosen = ordering[first_slot[:, :, None] + jnp.arange(ROWS_OWN, dtype=jnp.int32)[None, None, :]]
    gathered = values.reshape(block_count, TILE, F)[blocks[:, None, None], chosen]
    return jnp.transpose(gathered, (1, 0, 2, 3)).reshape(WROWS, F)


def draw_row_table(key, part):
    classes = row_classes(key)
    return classes


def draw_expert_owner(key, part):
    owners = owner_shifts(key)
    return owners


def draw_master(key, part):
    weights = base_weights(key)
    amplitude = drift_scales(key)
    key = jax.random.fold_in(key, 23)
    spread = jax.random.uniform(key, (WROWS, F), jnp.float32, -1.0, 1.0)
    widened = jnp.repeat(jnp.repeat(amplitude, TILE, axis=0), TILE, axis=1)
    return weights + widened * spread


def draw_synced(key, part):
    weights = base_weights(key)
    return weights.astype(jnp.bfloat16)


def draw_rollout(key, part):
    weights = base_weights(key)
    classes = row_classes(key)
    owners = owner_shifts(key)
    key = jax.random.fold_in(key, 25)
    jitter = 0.02 * jax.random.uniform(key, (WROWS, F), jnp.float32, -1.0, 1.0)
    return (rollout_order(weights, classes, owners) + jitter).astype(jnp.bfloat16)


def draw_amax_record(key, part):
    amplitude = drift_scales(key)
    key = jax.random.fold_in(key, 26)
    factor = jnp.exp(jax.random.uniform(key, (WROWS // TILE, F // TILE), jnp.float32, math.log(0.4), math.log(3.0)))
    return amplitude * factor


def raised(result, own_key, source, target, shards_of, factor):
    def block_of(axis_at):
        return (jnp.arange(result.shape[axis_at]) // (result.shape[axis_at] // shards_of)).reshape((-1,) + (1,) * (result.ndim - 1 - axis_at))

    one_side = jax.random.permutation(own_key, shards_of)[block_of(target)]
    far = (block_of(target) + shards_of // 2) % shards_of
    return jnp.where((block_of(source) == one_side) | (block_of(source) == far), factor * result, result)


def block_levels(stream_key, shape, pieces, low, largest):
    def one(axis_at, blocks):
        draws = jax.random.uniform(jax.random.fold_in(jax.random.fold_in(stream_key, 6), axis_at), (blocks,), jnp.float32, low / len(pieces), largest / len(pieces))
        return jnp.repeat(jnp.exp(draws), shape[axis_at] // blocks).reshape((-1,) + (1,) * (len(shape) - axis_at - 1))

    factor_of = one(*pieces[0])
    for cut in pieces[1:]:
        factor_of = factor_of * one(*cut)
    return factor_of


def gaussian(key, shape, scale, reach, cuts=(), held_as=jnp.bfloat16):
    entries = scale * jax.random.normal(key, shape, jnp.float32)
    if cuts:
        entries = entries * block_levels(key, shape, cuts, -0.22, 0.18)
    return jnp.clip(entries, -reach, reach).astype(held_as)


def gaussian_with(own_key, shape, scale, bound, cuts, heavy, kind=jnp.bfloat16):
    drawn = scale * jax.random.normal(own_key, shape, jnp.float32)
    if cuts:
        drawn = drawn * block_levels(own_key, shape, cuts, -0.22, 0.18)
    return jnp.clip(raised(drawn, jax.random.fold_in(own_key, 3), *heavy), -bound, bound).astype(kind)


def setup_inputs(seed: int = 0) -> dict:
    key_of = jax.random.split(jax.random.key(seed), 10)
    return {
        "gradients": gaussian_with(key_of[0], (N_DP, WROWS, F), 1.0, 6.0, ((0, 4), (1, 8)), (0, 2, 4, 2.0)),
        "master": draw_master(jax.random.fold_in(key_of[9], 71), 0),
        "moment_one": gaussian(key_of[2], (WROWS, F), 0.3, 4.0, ((0, 8), (1, 4)), jnp.float32),
        "moment_two": jnp.clip(jnp.exp(math.log(0.1) - 2.3025851 * jax.random.uniform(key_of[3], (WROWS, F), jnp.float32) ** block_levels(key_of[3], (WROWS, F), ((0, 8), (1, 4)), -0.2, 0.2)), 0.01, 0.1),
        "synced": draw_synced(jax.random.fold_in(key_of[9], 71), 0),
        "rollout": draw_rollout(jax.random.fold_in(key_of[9], 71), 0),
        "amax_record": draw_amax_record(jax.random.fold_in(key_of[9], 71), 0),
        "row_table": draw_row_table(jax.random.fold_in(key_of[9], 71), 0),
        "expert_owner": draw_expert_owner(jax.random.fold_in(key_of[9], 71), 0),
    }


beta_one = 0.9
beta_two = 0.95
bias_one = 1.0 - 0.9 ** 10
bias_two = 1.0 - 0.95 ** 10
step_size = 0.05
weight_decay = 0.1
adam_floor = 1e-08
code_limit = 448.0

def adam_step(master, moment_one, moment_two, gradient):
    new_one = beta_one * moment_one + (1.0 - beta_one) * gradient
    new_two = beta_two * moment_two + (1.0 - beta_two) * gradient * gradient
    update = new_one / bias_one / (jnp.sqrt(new_two / bias_two) + adam_floor)
    new_master = master - step_size * (update + weight_decay * master)
    return (new_master, new_one, new_two)

def owner_rows(row_table, expert_owner, blocks, owner_count):
    per_owner = TILE // owner_count
    ordering = jnp.argsort(row_table, stable=True).astype(jnp.int32)
    experts = (blocks * TILE // D).astype(jnp.int32)
    shifts = expert_owner[experts]
    owners = jnp.arange(owner_count, dtype=jnp.int32)
    first_slot = (owners[None, :] - shifts[:, None]) % owner_count * per_owner
    return ordering[first_slot[:, :, None] + jnp.arange(per_owner, dtype=jnp.int32)[None, None, :]]

def reference(gradients, master, moment_one, moment_two, synced, rollout, amax_record, row_table, expert_owner):
    summed = jnp.zeros(master.shape, jnp.float32)
    for replica in range(N_DP):
        summed = summed + gradients[replica].astype(jnp.float32)
    new_master, new_one, new_two = adam_step(master, moment_one, moment_two, summed / N_DP)
    difference = new_master - synced.astype(jnp.float32)
    block_count = WROWS // TILE
    tile_count = F // TILE
    tiled_delta = difference.reshape(block_count, TILE, tile_count, TILE)
    new_amax = lax.optimization_barrier(jnp.max(jnp.abs(tiled_delta), axis=(1, 3)))
    scales = amax_record / code_limit
    code_values = jnp.clip(tiled_delta / scales[:, None, :, None], -code_limit, code_limit).astype(jnp.bfloat16)
    restored = (code_values.astype(jnp.float32) * scales[:, None, :, None]).reshape(block_count, TILE, F)
    chosen = owner_rows(row_table, expert_owner, jnp.arange(block_count, dtype=jnp.int32), N_FSDP)
    picked_rows = restored[jnp.arange(block_count, dtype=jnp.int32)[:, None, None], chosen]
    regrouped = jnp.transpose(picked_rows, (1, 0, 2, 3)).reshape(WROWS, F)
    new_rollout = (rollout.astype(jnp.float32) + regrouped).astype(jnp.bfloat16)
    return (new_master, new_one, new_two, new_amax, new_rollout)
```

```python
import functools

import jax
import jax.numpy as jnp
from jax import lax
from jax.experimental import pallas as pl
from jax.experimental.pallas import tpu as pltpu
from jax.sharding import PartitionSpec as P

D = 7168
TILE = 128
MESH = pl.DeviceIdType.MESH

beta_one = 0.9
beta_two = 0.95
bias_one = 1.0 - 0.9**10
bias_two = 1.0 - 0.95**10
step_size = 0.05
weight_decay = 0.1
adam_floor = 1e-08
code_limit = 448.0


def adam_step(master, moment_one, moment_two, gradient):
    new_one = beta_one * moment_one + (1.0 - beta_one) * gradient
    new_two = beta_two * moment_two + (1.0 - beta_two) * gradient * gradient
    update = new_one / bias_one / (jnp.sqrt(new_two / bias_two) + adam_floor)
    new_master = master - step_size * (update + weight_decay * master)
    return (new_master, new_one, new_two)


HALVES = 2


def flipped(index, mask):
    out = index
    bit = 1
    while bit <= mask:
        if mask & bit:
            out = out + bit - 2 * bit * (lax.rem(index // bit, 2))
        bit *= 2
    return out


def fused_kernel(
    owners, grads, master, one, two, synced, rollout, amax, table, shifts,
    master_out, one_out, two_out, amax_out, rollout_out,
    far_own, near_own, far_sib, near_sib, far_sum, far_in,
    master_v, one_v, two_v, synced_v, rollout_v,
    master_w, one_w, two_w, rollout_w, packed, arrived,
    load_sem, far_send, far_recv, near_send, near_recv, x_send, x_recv, row_send, row_recv, store_sem,
):
    d = lax.axis_index("dp")
    f = lax.axis_index("fsdp")
    rows, cols = master_v.shape
    blocks = rows // TILE
    width = cols // HALVES
    part = TILE // owners
    chunks = [(b, h) for b in range(blocks) for h in range(HALVES)]
    sib = flipped(d, 1)
    opp = flipped(d, 2)
    opp_sib = flipped(d, 3)

    barrier = pltpu.get_barrier_semaphore()
    pl.semaphore_signal(barrier, inc=1, device_id={"dp": sib}, device_id_type=MESH)
    pl.semaphore_signal(barrier, inc=1, device_id={"dp": opp}, device_id_type=MESH)
    for j in range(1, owners):
        pl.semaphore_signal(barrier, inc=1, device_id={"fsdp": flipped(f, j)}, device_id_type=MESH)

    def columns(q):
        return pl.ds(pl.multiple_of(q * cols, cols), cols)

    loads = [
        pltpu.make_async_copy(src, dst, load_sem.at[n])
        for n, (src, dst) in enumerate([
            (grads.at[:, columns(opp)], far_own),
            (grads.at[:, columns(d)], near_own),
            (one, one_v),
            (two, two_v),
            (master, master_v),
            (synced, synced_v),
            (rollout, rollout_v),
        ])
    ]
    for load in loads:
        load.start()

    ti = lax.broadcasted_iota(jnp.int32, (TILE, TILE), 0)
    tj = lax.broadcasted_iota(jnp.int32, (TILE, TILE), 1)
    key_row = table[...] * TILE + lax.broadcasted_iota(jnp.int32, (1, TILE), 1)
    key_mat = jnp.broadcast_to(key_row, (TILE, TILE)).astype(jnp.float32)
    key_col = jnp.sum(jnp.where(ti == tj, key_mat, 0.0), axis=1, keepdims=True)
    rank = jnp.sum(jnp.where(key_col < key_mat, 1.0, 0.0), axis=0, keepdims=True).astype(jnp.int32)

    def chooser(b):
        shift = shifts[((f * blocks + b) * TILE) // D]
        dest = (rank + shift * part) & (TILE - 1)
        return jnp.where(ti == dest, 1.0, 0.0).astype(jnp.bfloat16)

    pl.semaphore_wait(barrier, owners + 1)

    def at(ref, b, h):
        return ref.at[pl.ds(b * TILE, TILE), pl.ds(h * width, width)]

    far_copies = []
    for n, (b, h) in enumerate(chunks):
        source = pl.multiple_of(opp_sib * cols + h * width, width)
        copy = pltpu.make_async_remote_copy(
            src_ref=grads.at[pl.ds(b * TILE, TILE), pl.ds(source, width)],
            dst_ref=at(far_sib, b, h),
            send_sem=far_send.at[n], recv_sem=far_recv.at[n],
            device_id={"dp": sib}, device_id_type=MESH,
        )
        copy.start()
        far_copies.append(copy)
    near_copies = []
    for b in range(blocks):
        copy = pltpu.make_async_remote_copy(
            src_ref=grads.at[pl.ds(b * TILE, TILE), columns(sib)],
            dst_ref=near_sib.at[pl.ds(b * TILE, TILE), :],
            send_sem=near_send.at[b], recv_sem=near_recv.at[b],
            device_id={"dp": sib}, device_id_type=MESH,
        )
        copy.start()
        near_copies.append(copy)

    x_copies = []
    loads[0].wait()
    for n, (b, h) in enumerate(chunks):
        far_copies[n].wait_recv()
        mine = at(far_own, b, h)[...].astype(jnp.float32)
        theirs = at(far_sib, b, h)[...].astype(jnp.float32)
        at(far_sum, b, h)[...] = (mine + theirs).astype(jnp.bfloat16)
        copy = pltpu.make_async_remote_copy(
            src_ref=at(far_sum, b, h), dst_ref=at(far_in, b, h),
            send_sem=x_send.at[n], recv_sem=x_recv.at[n],
            device_id={"dp": opp}, device_id_type=MESH,
        )
        copy.start()
        x_copies.append(copy)

    for load in loads[1:]:
        load.wait()

    row_copies = []
    stores = []
    choose = None
    for n, (b, h) in enumerate(chunks):
        if h == 0:
            near_copies[b].wait_recv()
            choose = chooser(b)
        x_copies[n].wait_recv()
        summed = (
            at(near_own, b, h)[...].astype(jnp.float32)
            + at(near_sib, b, h)[...].astype(jnp.float32)
            + at(far_in, b, h)[...].astype(jnp.float32)
        )
        new_master, new_one, new_two = adam_step(
            at(master_v, b, h)[...], at(one_v, b, h)[...], at(two_v, b, h)[...], summed / 4.0
        )
        at(master_w, b, h)[...] = new_master
        at(one_w, b, h)[...] = new_one
        at(two_w, b, h)[...] = new_two
        delta = new_master - at(synced_v, b, h)[...].astype(jnp.float32)
        restored = []
        for k in range(width // TILE):
            t = h * (width // TILE) + k
            piece = delta[:, k * TILE : (k + 1) * TILE]
            top = jnp.max(jnp.max(jnp.abs(piece), axis=0, keepdims=True), axis=1, keepdims=True)
            amax_out[b : b + 1, t : t + 1] = top
            limit = amax[b, t] / code_limit * code_limit
            restored.append(jnp.clip(piece, -limit, limit).astype(jnp.bfloat16))
        restored = jnp.concatenate(restored, axis=1)
        packed[b, :, pl.ds(h * width, width)] = jnp.dot(
            choose, restored, preferred_element_type=jnp.float32
        ).astype(jnp.bfloat16)
        for j in sorted(range(1, owners), key=lambda j: -(j // 2)):
            target = flipped(f, j)
            copy = pltpu.make_async_remote_copy(
                src_ref=packed.at[b, pl.ds(pl.multiple_of(target * part, part), part), pl.ds(h * width, width)],
                dst_ref=arrived.at[f, b, :, pl.ds(h * width, width)],
                send_sem=row_send.at[n, j - 1], recv_sem=row_recv.at[n, j - 1],
                device_id={"fsdp": target}, device_id_type=MESH,
            )
            copy.start()
            row_copies.append((n, copy))
        arrived[f, b, :, pl.ds(h * width, width)] = packed[
            b, pl.ds(pl.multiple_of(f * part, part), part), pl.ds(h * width, width)
        ]
        if h == HALVES - 1:
            for m, (src, dst) in enumerate([(master_w, master_out), (one_w, one_out), (two_w, two_out)]):
                cut = pl.ds(b * TILE, TILE)
                store = pltpu.make_async_copy(src.at[cut, :], dst.at[cut, :], store_sem.at[m * blocks + b])
                store.start()
                stores.append(store)

    for n, (b, h) in enumerate(chunks):
        for m, copy in row_copies:
            if m == n:
                copy.wait_recv()
        cut = pl.ds(h * width, width)
        rollout_w[:, b, :, cut] = (
            rollout_v[:, b, :, cut].astype(jnp.float32) + arrived[:, b, :, cut].astype(jnp.float32)
        ).astype(jnp.bfloat16)
        if h == HALVES - 1:
            store = pltpu.make_async_copy(
                rollout_w.at[:, b], rollout_out.at[:, b], store_sem.at[3 * blocks + b]
            )
            store.start()
            stores.append(store)

    for copy in far_copies + near_copies + x_copies + [c for _, c in row_copies]:
        copy.wait_send()
    for store in stores:
        store.wait()


def fused_body(gradients, master, one, two, synced, rollout, amax, table, shifts):
    owners = lax.axis_size("fsdp")
    rows, cols = master.shape
    blocks = rows // TILE
    part = TILE // owners
    n = blocks * HALVES
    f32, bf16 = jnp.float32, jnp.bfloat16
    hbm = pl.BlockSpec(memory_space=pl.ANY)
    vmem = pl.BlockSpec(memory_space=pltpu.VMEM)
    smem = pl.BlockSpec(memory_space=pltpu.SMEM)
    grouped = (owners, blocks, part, cols)
    whole = (rows, cols)
    dma = pltpu.SemaphoreType.DMA
    outs = pl.pallas_call(
        functools.partial(fused_kernel, owners),
        out_shape=(
            jax.ShapeDtypeStruct(whole, f32),
            jax.ShapeDtypeStruct(whole, f32),
            jax.ShapeDtypeStruct(whole, f32),
            jax.ShapeDtypeStruct(amax.shape, f32),
            jax.ShapeDtypeStruct(grouped, bf16),
        ),
        in_specs=[hbm] * 6 + [smem, vmem, smem],
        out_specs=(hbm, hbm, hbm, vmem, hbm),
        scratch_shapes=(
            [pltpu.VMEM(whole, bf16)] * 6
            + [pltpu.VMEM(whole, f32)] * 3
            + [pltpu.VMEM(whole, bf16), pltpu.VMEM(grouped, bf16)]
            + [pltpu.VMEM(whole, f32)] * 3
            + [pltpu.VMEM(grouped, bf16), pltpu.VMEM((blocks, TILE, cols), bf16), pltpu.VMEM(grouped, bf16)]
            + [
                dma((7,)), dma((n,)), dma((n,)), dma((blocks,)), dma((blocks,)), dma((n,)), dma((n,)),
                dma((n, owners - 1)), dma((n, owners - 1)), dma((4 * blocks,)),
            ]
        ),
        compiler_params=pltpu.CompilerParams(
            collective_id=0, has_side_effects=True, vmem_limit_bytes=32 * 1024 * 1024
        ),
    )(
        gradients[0], master, one, two, synced, rollout.reshape(grouped), amax,
        table.reshape(1, TILE), shifts,
    )
    return outs[0], outs[1], outs[2], outs[3], outs[4].reshape(whole)


def owner_rows(row_table, expert_owner, blocks, owner_count):
    per_owner = TILE // owner_count
    ordering = jnp.argsort(row_table, stable=True)
    experts = blocks * TILE // D
    shifts = expert_owner[experts]
    owners = jnp.arange(owner_count, dtype=jnp.int32)
    first_slot = (owners[None, :] - shifts[:, None]) % owner_count * per_owner
    return ordering[first_slot[:, :, None] + jnp.arange(per_owner, dtype=jnp.int32)[None, None, :]]


def plain_body(
    gradients, master, moment_one, moment_two, synced, rollout, amax_record, row_table, expert_owner
):
    owner_count = lax.axis_size("fsdp")
    replica_count = lax.axis_size("dp")
    row_count, column_count = master.shape
    summed = lax.psum_scatter(
        gradients[0].astype(jnp.float32).astype(jnp.bfloat16), "dp", scatter_dimension=1, tiled=True
    ).astype(jnp.float32)
    new_master, new_one, new_two = adam_step(master, moment_one, moment_two, summed / replica_count)
    difference = new_master - synced.astype(jnp.float32)
    block_count = row_count // TILE
    tile_count = column_count // TILE
    tiled_delta = difference.reshape(block_count, TILE, tile_count, TILE)
    new_amax = jnp.max(jnp.abs(tiled_delta), axis=(1, 3))
    scales = amax_record / code_limit
    code_values = (
        jnp.clip(tiled_delta / scales[:, None, :, None], -code_limit, code_limit)
        .astype(jnp.bfloat16)
        .reshape(block_count, TILE, column_count)
    )
    blocks = lax.axis_index("fsdp") * block_count + jnp.arange(block_count, dtype=jnp.int32)
    chosen = owner_rows(row_table, expert_owner, blocks, owner_count)
    per_owner = TILE // owner_count
    ordered = code_values[jnp.arange(block_count, dtype=jnp.int32)[:, None, None], chosen]
    outgoing = jnp.transpose(ordered, (1, 0, 2, 3)).reshape(
        owner_count, block_count * per_owner, column_count
    )
    spread = jnp.broadcast_to(scales[None], (owner_count, block_count, tile_count))
    incoming, scales_in = (
        lax.all_to_all(outgoing, "fsdp", split_axis=0, concat_axis=0, tiled=True),
        lax.all_to_all(
            spread.astype(jnp.bfloat16), "fsdp", split_axis=0, concat_axis=0, tiled=True
        ).astype(spread.dtype),
    )
    restored = (
        incoming.reshape(owner_count, block_count, per_owner, tile_count, TILE).astype(jnp.float32)
        * scales_in[:, :, None, :, None]
    )
    new_rollout = (rollout.astype(jnp.float32) + restored.reshape(row_count, column_count)).astype(
        jnp.bfloat16
    )
    return (new_master, new_one, new_two, new_amax, new_rollout)


def solution(mesh):
    sizes = dict(mesh.shape)
    fits = sizes["dp"] == 4 and sizes["fsdp"] == 8
    return jax.shard_map(
        fused_body if fits else plain_body,
        mesh=mesh,
        in_specs=(
            P("dp", "fsdp", None),
            P("fsdp", "dp"),
            P("fsdp", "dp"),
            P("fsdp", "dp"),
            P("fsdp", "dp"),
            P("fsdp", "dp"),
            P("fsdp", "dp"),
            P(),
            P(),
        ),
        out_specs=(
            P("fsdp", "dp"),
            P("fsdp", "dp"),
            P("fsdp", "dp"),
            P("fsdp", "dp"),
            P("fsdp", "dp"),
        ),
        check_vma=False,
    )
```

```python
import functools

import jax
import jax.numpy as jnp
from jax import lax
from jax.experimental import pallas as pl
from jax.experimental.pallas import tpu as pltpu
from jax.sharding import PartitionSpec as P

D = 7168
TILE = 128
MESH = pl.DeviceIdType.MESH

beta_one = 0.9
beta_two = 0.95
bias_one = 1.0 - 0.9**10
bias_two = 1.0 - 0.95**10
step_size = 0.05
weight_decay = 0.1
adam_floor = 1e-08
code_limit = 448.0


def adam_step(master, moment_one, moment_two, gradient):
    new_one = beta_one * moment_one + (1.0 - beta_one) * gradient
    new_two = beta_two * moment_two + (1.0 - beta_two) * gradient * gradient
    update = new_one / bias_one / (jnp.sqrt(new_two / bias_two) + adam_floor)
    new_master = master - step_size * (update + weight_decay * master)
    return (new_master, new_one, new_two)


HALVES = 2


def flipped(index, mask):
    out = index
    bit = 1
    while bit <= mask:
        if mask & bit:
            out = out + bit - 2 * bit * (lax.rem(index // bit, 2))
        bit *= 2
    return out


def fused_kernel(
    owners, grads, master, one, two, synced, rollout, amax_h, table_h, shifts,
    master_w, one_w, two_w, amax_out, rollout_w,
    far_own, near_own, far_sib, near_sib, far_sum, far_in,
    master_v, one_v, two_v, synced_v, rollout_v, packed, arrived, amax, table,
    load_sem, far_send, far_recv, near_send, near_recv, x_send, x_recv, row_send, row_recv,
):
    d = lax.axis_index("dp")
    f = lax.axis_index("fsdp")
    rows, cols = master_v.shape
    blocks = rows // TILE
    width = cols // HALVES
    part = TILE // owners
    chunks = [(b, h) for b in range(blocks) for h in range(HALVES)]
    sib = flipped(d, 1)
    opp = flipped(d, 2)
    opp_sib = flipped(d, 3)

    barrier = pltpu.get_barrier_semaphore()
    pl.semaphore_signal(barrier, inc=1, device_id={"dp": sib}, device_id_type=MESH)
    pl.semaphore_signal(barrier, inc=1, device_id={"dp": opp}, device_id_type=MESH)
    for j in range(1, owners):
        pl.semaphore_signal(barrier, inc=1, device_id={"fsdp": flipped(f, j)}, device_id_type=MESH)

    def columns(q):
        return pl.ds(pl.multiple_of(q * cols, cols), cols)

    loads = [
        pltpu.make_async_copy(src, dst, load_sem.at[n])
        for n, (src, dst) in enumerate([
            (table_h, table),
            (amax_h, amax),
            (grads.at[:, columns(opp)], far_own),
            (grads.at[:, columns(d)], near_own),
            (one, one_v),
            (two, two_v),
            (master, master_v),
            (synced, synced_v),
            (rollout, rollout_v),
        ])
    ]
    for load in loads:
        load.start()
    def chooser(b):
        shift = shifts[((f * blocks + b) * TILE) // D]
        dest = (rank + shift * part) & (TILE - 1)
        return jnp.where(ti == dest, 1.0, 0.0).astype(jnp.bfloat16)

    pl.semaphore_wait(barrier, owners + 1)

    def at(ref, b, h):
        return ref.at[pl.ds(b * TILE, TILE), pl.ds(h * width, width)]

    far_copies = []
    for n, (b, h) in enumerate(chunks):
        source = pl.multiple_of(opp_sib * cols + h * width, width)
        copy = pltpu.make_async_remote_copy(
            src_ref=grads.at[pl.ds(b * TILE, TILE), pl.ds(source, width)],
            dst_ref=at(far_sib, b, h),
            send_sem=far_send.at[n], recv_sem=far_recv.at[n],
            device_id={"dp": sib}, device_id_type=MESH,
        )
        copy.start()
        far_copies.append(copy)
    near_copies = []
    for b in range(blocks):
        copy = pltpu.make_async_remote_copy(
            src_ref=grads.at[pl.ds(b * TILE, TILE), columns(sib)],
            dst_ref=near_sib.at[pl.ds(b * TILE, TILE), :],
            send_sem=near_send.at[b], recv_sem=near_recv.at[b],
            device_id={"dp": sib}, device_id_type=MESH,
        )
        copy.start()
        near_copies.append(copy)

    x_copies = []
    loads[2].wait()
    for n, (b, h) in enumerate(chunks):
        far_copies[n].wait_recv()
        mine = at(far_own, b, h)[...].astype(jnp.float32)
        theirs = at(far_sib, b, h)[...].astype(jnp.float32)
        at(far_sum, b, h)[...] = (mine + theirs).astype(jnp.bfloat16)
        copy = pltpu.make_async_remote_copy(
            src_ref=at(far_sum, b, h), dst_ref=at(far_in, b, h),
            send_sem=x_send.at[n], recv_sem=x_recv.at[n],
            device_id={"dp": opp}, device_id_type=MESH,
        )
        copy.start()
        x_copies.append(copy)

    for load in loads[:2]:
        load.wait()

    ti = lax.broadcasted_iota(jnp.int32, (TILE, TILE), 0)
    tj = lax.broadcasted_iota(jnp.int32, (TILE, TILE), 1)
    key_row = table[...] * TILE + lax.broadcasted_iota(jnp.int32, (1, TILE), 1)
    key_mat = jnp.broadcast_to(key_row, (TILE, TILE)).astype(jnp.float32)
    key_col = jnp.sum(jnp.where(ti == tj, key_mat, 0.0), axis=1, keepdims=True)
    rank = jnp.sum(jnp.where(key_col < key_mat, 1.0, 0.0), axis=0, keepdims=True).astype(jnp.int32)
    for load in loads[3:]:
        load.wait()

    row_copies = []
    choose = None
    for n, (b, h) in enumerate(chunks):
        if h == 0:
            near_copies[b].wait_recv()
            choose = chooser(b)
        x_copies[n].wait_recv()
        summed = (
            at(near_own, b, h)[...].astype(jnp.float32)
            + at(near_sib, b, h)[...].astype(jnp.float32)
            + at(far_in, b, h)[...].astype(jnp.float32)
        )
        new_master, new_one, new_two = adam_step(
            at(master_v, b, h)[...], at(one_v, b, h)[...], at(two_v, b, h)[...], summed / 4.0
        )
        at(master_w, b, h)[...] = new_master
        at(one_w, b, h)[...] = new_one
        at(two_w, b, h)[...] = new_two
        delta = new_master - at(synced_v, b, h)[...].astype(jnp.float32)
        restored = []
        for k in range(width // TILE):
            t = h * (width // TILE) + k
            piece = delta[:, k * TILE : (k + 1) * TILE]
            top = jnp.max(jnp.max(jnp.abs(piece), axis=0, keepdims=True), axis=1, keepdims=True)
            amax_out[b : b + 1, t : t + 1] = top
            limit = amax[b, t] / code_limit * code_limit
            restored.append(jnp.clip(piece, -limit, limit).astype(jnp.bfloat16))
        restored = jnp.concatenate(restored, axis=1)
        packed[b, :, pl.ds(h * width, width)] = jnp.dot(
            choose, restored, preferred_element_type=jnp.float32
        ).astype(jnp.bfloat16)
        for j in sorted(range(1, owners), key=lambda j: -(j // 2)):
            target = flipped(f, j)
            copy = pltpu.make_async_remote_copy(
                src_ref=packed.at[b, pl.ds(pl.multiple_of(target * part, part), part), pl.ds(h * width, width)],
                dst_ref=arrived.at[f, b, :, pl.ds(h * width, width)],
                send_sem=row_send.at[n, j - 1], recv_sem=row_recv.at[n, j - 1],
                device_id={"fsdp": target}, device_id_type=MESH,
            )
            copy.start()
            row_copies.append((n, copy))
        arrived[f, b, :, pl.ds(h * width, width)] = packed[
            b, pl.ds(pl.multiple_of(f * part, part), part), pl.ds(h * width, width)
        ]

    for n, (b, h) in enumerate(chunks):
        for m, copy in row_copies:
            if m == n:
                copy.wait_recv()
        cut = pl.ds(h * width, width)
        rollout_w[:, b, :, cut] = (
            rollout_v[:, b, :, cut].astype(jnp.float32) + arrived[:, b, :, cut].astype(jnp.float32)
        ).astype(jnp.bfloat16)

    for copy in far_copies + near_copies + x_copies + [c for _, c in row_copies]:
        copy.wait_send()


def write_kernel(*refs):
    count = len(refs) // 2
    sem = refs[-1]
    copies = [pltpu.make_async_copy(refs[n], refs[count + n], sem.at[n]) for n in range(count)]
    for copy in copies:
        copy.start()
    for copy in copies:
        copy.wait()


def fused_body(gradients, master, one, two, synced, rollout, amax, table, shifts):
    owners = lax.axis_size("fsdp")
    rows, cols = master.shape
    blocks = rows // TILE
    part = TILE // owners
    n = blocks * HALVES
    f32, bf16 = jnp.float32, jnp.bfloat16
    hbm = pl.BlockSpec(memory_space=pltpu.HBM)
    vmem = pl.BlockSpec(memory_space=pltpu.VMEM)
    grouped = (owners, blocks, part, cols)
    whole = (rows, cols)
    dma = pltpu.SemaphoreType.DMA
    results = (
        jax.ShapeDtypeStruct(whole, f32),
        jax.ShapeDtypeStruct(whole, f32),
        jax.ShapeDtypeStruct(whole, f32),
        jax.ShapeDtypeStruct(amax.shape, f32),
        jax.ShapeDtypeStruct(grouped, bf16),
    )
    outs = pl.pallas_call(
        functools.partial(fused_kernel, owners),
        out_shape=tuple(pltpu.VMEM(r.shape, r.dtype) for r in results),
        in_specs=[hbm] * 8 + [pl.BlockSpec(memory_space=pltpu.SMEM)],
        out_specs=(vmem,) * 5,
        scratch_shapes=(
            [pltpu.VMEM(whole, bf16)] * 6
            + [pltpu.VMEM(whole, f32)] * 3
            + [pltpu.VMEM(whole, bf16), pltpu.VMEM(grouped, bf16)]
            + [pltpu.VMEM((blocks, TILE, cols), bf16), pltpu.VMEM(grouped, bf16)]
            + [pltpu.SMEM(amax.shape, f32), pltpu.VMEM((1, TILE), jnp.int32)]
            + [
                dma((9,)), dma((n,)), dma((n,)), dma((blocks,)), dma((blocks,)), dma((n,)), dma((n,)),
                dma((n, owners - 1)), dma((n, owners - 1)),
            ]
        ),
        compiler_params=pltpu.CompilerParams(
            collective_id=0, has_side_effects=True, vmem_limit_bytes=32 * 1024 * 1024
        ),
    )(*[
        pltpu.with_memory_space_constraint(x, pltpu.HBM)
        for x in (
            gradients[0], master, one, two, synced, rollout.reshape(grouped), amax,
            table.reshape(1, TILE),
        )
    ], shifts)
    outs = pl.pallas_call(
        write_kernel,
        out_shape=results,
        in_specs=[vmem] * 5,
        out_specs=(hbm,) * 5,
        scratch_shapes=[dma((5,))],
    )(*outs)
    return outs[0], outs[1], outs[2], outs[3], outs[4].reshape(whole)


def owner_rows(row_table, expert_owner, blocks, owner_count):
    per_owner = TILE // owner_count
    ordering = jnp.argsort(row_table, stable=True)
    experts = blocks * TILE // D
    shifts = expert_owner[experts]
    owners = jnp.arange(owner_count, dtype=jnp.int32)
    first_slot = (owners[None, :] - shifts[:, None]) % owner_count * per_owner
    return ordering[first_slot[:, :, None] + jnp.arange(per_owner, dtype=jnp.int32)[None, None, :]]


def plain_body(
    gradients, master, moment_one, moment_two, synced, rollout, amax_record, row_table, expert_owner
):
    owner_count = lax.axis_size("fsdp")
    replica_count = lax.axis_size("dp")
    row_count, column_count = master.shape
    summed = lax.psum_scatter(
        gradients[0].astype(jnp.float32).astype(jnp.bfloat16), "dp", scatter_dimension=1, tiled=True
    ).astype(jnp.float32)
    new_master, new_one, new_two = adam_step(master, moment_one, moment_two, summed / replica_count)
    difference = new_master - synced.astype(jnp.float32)
    block_count = row_count // TILE
    tile_count = column_count // TILE
    tiled_delta = difference.reshape(block_count, TILE, tile_count, TILE)
    new_amax = jnp.max(jnp.abs(tiled_delta), axis=(1, 3))
    scales = amax_record / code_limit
    code_values = (
        jnp.clip(tiled_delta / scales[:, None, :, None], -code_limit, code_limit)
        .astype(jnp.bfloat16)
        .reshape(block_count, TILE, column_count)
    )
    blocks = lax.axis_index("fsdp") * block_count + jnp.arange(block_count, dtype=jnp.int32)
    chosen = owner_rows(row_table, expert_owner, blocks, owner_count)
    per_owner = TILE // owner_count
    ordered = code_values[jnp.arange(block_count, dtype=jnp.int32)[:, None, None], chosen]
    outgoing = jnp.transpose(ordered, (1, 0, 2, 3)).reshape(
        owner_count, block_count * per_owner, column_count
    )
    spread = jnp.broadcast_to(scales[None], (owner_count, block_count, tile_count))
    incoming, scales_in = (
        lax.all_to_all(outgoing, "fsdp", split_axis=0, concat_axis=0, tiled=True),
        lax.all_to_all(
            spread.astype(jnp.bfloat16), "fsdp", split_axis=0, concat_axis=0, tiled=True
        ).astype(spread.dtype),
    )
    restored = (
        incoming.reshape(owner_count, block_count, per_owner, tile_count, TILE).astype(jnp.float32)
        * scales_in[:, :, None, :, None]
    )
    new_rollout = (rollout.astype(jnp.float32) + restored.reshape(row_count, column_count)).astype(
        jnp.bfloat16
    )
    return (new_master, new_one, new_two, new_amax, new_rollout)


def solution(mesh):
    sizes = dict(mesh.shape)
    fits = sizes["dp"] == 4 and sizes["fsdp"] == 8
    return jax.shard_map(
        fused_body if fits else plain_body,
        mesh=mesh,
        in_specs=(
            P("dp", "fsdp", None),
            P("fsdp", "dp"),
            P("fsdp", "dp"),
            P("fsdp", "dp"),
            P("fsdp", "dp"),
            P("fsdp", "dp"),
            P("fsdp", "dp"),
            P(),
            P(),
        ),
        out_specs=(
            P("fsdp", "dp"),
            P("fsdp", "dp"),
            P("fsdp", "dp"),
            P("fsdp", "dp"),
            P("fsdp", "dp"),
        ),
        check_vma=False,
    )
```

```python
import functools

import jax
import jax.numpy as jnp
from jax import lax
from jax.experimental import pallas as pl
from jax.experimental.pallas import tpu as pltpu
from jax.sharding import PartitionSpec as P

D = 7168
TILE = 128
MESH = pl.DeviceIdType.MESH

beta_one = 0.9
beta_two = 0.95
bias_one = 1.0 - 0.9**10
bias_two = 1.0 - 0.95**10
step_size = 0.05
weight_decay = 0.1
adam_floor = 1e-08
code_limit = 448.0


def adam_step(master, moment_one, moment_two, gradient):
    new_one = beta_one * moment_one + (1.0 - beta_one) * gradient
    new_two = beta_two * moment_two + (1.0 - beta_two) * gradient * gradient
    update = new_one / bias_one / (jnp.sqrt(new_two / bias_two) + adam_floor)
    new_master = master - step_size * (update + weight_decay * master)
    return (new_master, new_one, new_two)


HALVES = 2


def flipped(index, mask):
    out = index
    bit = 1
    while bit <= mask:
        if mask & bit:
            out = out + bit - 2 * bit * (lax.rem(index // bit, 2))
        bit *= 2
    return out


def fused_kernel(
    owners, grads, master, one, two, synced, rollout, amax_h, table_h, shifts,
    master_w, one_w, two_w, amax_out, rollout_w,
    far_own, near_own, far_sib, near_sib, far_sum, far_in,
    master_v, one_v, two_v, synced_v, rollout_v, packed, arrived, amax, table,
    load_sem, far_send, far_recv, near_send, near_recv, x_send, x_recv, row_send, row_recv,
):
    d = lax.axis_index("dp")
    f = lax.axis_index("fsdp")
    rows, cols = master_v.shape
    blocks = rows // TILE
    width = cols // HALVES
    part = TILE // owners
    chunks = [(b, h) for b in range(blocks) for h in range(HALVES)]
    sib = flipped(d, 1)
    opp = flipped(d, 2)
    opp_sib = flipped(d, 3)

    barrier = pltpu.get_barrier_semaphore()
    pl.semaphore_signal(barrier, inc=1, device_id={"dp": sib}, device_id_type=MESH)
    pl.semaphore_signal(barrier, inc=1, device_id={"dp": opp}, device_id_type=MESH)
    for j in range(1, owners):
        pl.semaphore_signal(barrier, inc=1, device_id={"fsdp": flipped(f, j)}, device_id_type=MESH)

    def columns(q):
        return pl.ds(pl.multiple_of(q * cols, cols), cols)

    loads = [
        pltpu.make_async_copy(src, dst, load_sem.at[n])
        for n, (src, dst) in enumerate([
            (table_h, table),
            (amax_h, amax),
            (grads.at[:, columns(opp)], far_own),
            (grads.at[:, columns(d)], near_own),
            (one, one_v),
            (two, two_v),
            (master, master_v),
            (synced, synced_v),
            (rollout, rollout_v),
        ])
    ]
    for load in loads[:4]:
        load.start()

    def chooser(b):
        shift = shifts[((f * blocks + b) * TILE) // D]
        dest = (rank + shift * part) & (TILE - 1)
        return jnp.where(ti == dest, 1.0, 0.0).astype(jnp.bfloat16)

    pl.semaphore_wait(barrier, owners + 1)

    def at(ref, b, h):
        return ref.at[pl.ds(b * TILE, TILE), pl.ds(h * width, width)]

    far_copies = []
    for n, (b, h) in enumerate(chunks):
        source = pl.multiple_of(opp_sib * cols + h * width, width)
        copy = pltpu.make_async_remote_copy(
            src_ref=grads.at[pl.ds(b * TILE, TILE), pl.ds(source, width)],
            dst_ref=at(far_sib, b, h),
            send_sem=far_send.at[n], recv_sem=far_recv.at[n],
            device_id={"dp": sib}, device_id_type=MESH,
        )
        copy.start()
        far_copies.append(copy)
    near_copies = []
    for b in range(blocks):
        copy = pltpu.make_async_remote_copy(
            src_ref=grads.at[pl.ds(b * TILE, TILE), columns(sib)],
            dst_ref=near_sib.at[pl.ds(b * TILE, TILE), :],
            send_sem=near_send.at[b], recv_sem=near_recv.at[b],
            device_id={"dp": sib}, device_id_type=MESH,
        )
        copy.start()
        near_copies.append(copy)

    for load in loads[4:]:
        load.start()

    x_copies = []
    loads[2].wait()
    for n, (b, h) in enumerate(chunks):
        far_copies[n].wait_recv()
        mine = at(far_own, b, h)[...].astype(jnp.float32)
        theirs = at(far_sib, b, h)[...].astype(jnp.float32)
        at(far_sum, b, h)[...] = (mine + theirs).astype(jnp.bfloat16)
        copy = pltpu.make_async_remote_copy(
            src_ref=at(far_sum, b, h), dst_ref=at(far_in, b, h),
            send_sem=x_send.at[n], recv_sem=x_recv.at[n],
            device_id={"dp": opp}, device_id_type=MESH,
        )
        copy.start()
        x_copies.append(copy)

    for load in loads[:2]:
        load.wait()

    ti = lax.broadcasted_iota(jnp.int32, (TILE, TILE), 0)
    tj = lax.broadcasted_iota(jnp.int32, (TILE, TILE), 1)
    key_row = table[...] * TILE + lax.broadcasted_iota(jnp.int32, (1, TILE), 1)
    key_mat = jnp.broadcast_to(key_row, (TILE, TILE)).astype(jnp.float32)
    key_col = jnp.sum(jnp.where(ti == tj, key_mat, 0.0), axis=1, keepdims=True)
    rank = jnp.sum(jnp.where(key_col < key_mat, 1.0, 0.0), axis=0, keepdims=True).astype(jnp.int32)
    for load in loads[3:]:
        load.wait()

    row_copies = []
    choose = None
    for n, (b, h) in enumerate(chunks):
        if h == 0:
            near_copies[b].wait_recv()
            choose = chooser(b)
        x_copies[n].wait_recv()
        summed = (
            at(near_own, b, h)[...].astype(jnp.float32)
            + at(near_sib, b, h)[...].astype(jnp.float32)
            + at(far_in, b, h)[...].astype(jnp.float32)
        )
        new_master, new_one, new_two = adam_step(
            at(master_v, b, h)[...], at(one_v, b, h)[...], at(two_v, b, h)[...], summed / 4.0
        )
        at(master_w, b, h)[...] = new_master
        at(one_w, b, h)[...] = new_one
        at(two_w, b, h)[...] = new_two
        delta = new_master - at(synced_v, b, h)[...].astype(jnp.float32)
        restored = []
        for k in range(width // TILE):
            t = h * (width // TILE) + k
            piece = delta[:, k * TILE : (k + 1) * TILE]
            top = jnp.max(jnp.max(jnp.abs(piece), axis=0, keepdims=True), axis=1, keepdims=True)
            amax_out[b : b + 1, t : t + 1] = top
            limit = amax[b, t] / code_limit * code_limit
            restored.append(jnp.clip(piece, -limit, limit).astype(jnp.bfloat16))
        restored = jnp.concatenate(restored, axis=1)
        packed[b, :, pl.ds(h * width, width)] = jnp.dot(
            choose, restored, preferred_element_type=jnp.float32
        ).astype(jnp.bfloat16)
        for j in sorted(range(1, owners), key=lambda j: -(j // 2)):
            target = flipped(f, j)
            copy = pltpu.make_async_remote_copy(
                src_ref=packed.at[b, pl.ds(pl.multiple_of(target * part, part), part), pl.ds(h * width, width)],
                dst_ref=arrived.at[f, b, :, pl.ds(h * width, width)],
                send_sem=row_send.at[n, j - 1], recv_sem=row_recv.at[n, j - 1],
                device_id={"fsdp": target}, device_id_type=MESH,
            )
            copy.start()
            row_copies.append((n, copy))
        arrived[f, b, :, pl.ds(h * width, width)] = packed[
            b, pl.ds(pl.multiple_of(f * part, part), part), pl.ds(h * width, width)
        ]

    for n, (b, h) in enumerate(chunks):
        for m, copy in row_copies:
            if m == n:
                copy.wait_recv()
        cut = pl.ds(h * width, width)
        rollout_w[:, b, :, cut] = (
            rollout_v[:, b, :, cut].astype(jnp.float32) + arrived[:, b, :, cut].astype(jnp.float32)
        ).astype(jnp.bfloat16)

    for copy in far_copies + near_copies + x_copies + [c for _, c in row_copies]:
        copy.wait_send()


def write_kernel(*refs):
    count = len(refs) // 2
    sem = refs[-1]
    copies = [pltpu.make_async_copy(refs[n], refs[count + n], sem.at[n]) for n in range(count)]
    for copy in copies:
        copy.start()
    for copy in copies:
        copy.wait()


def fused_body(gradients, master, one, two, synced, rollout, amax, table, shifts):
    owners = lax.axis_size("fsdp")
    rows, cols = master.shape
    blocks = rows // TILE
    part = TILE // owners
    n = blocks * HALVES
    f32, bf16 = jnp.float32, jnp.bfloat16
    hbm = pl.BlockSpec(memory_space=pltpu.HBM)
    vmem = pl.BlockSpec(memory_space=pltpu.VMEM)
    grouped = (owners, blocks, part, cols)
    whole = (rows, cols)
    dma = pltpu.SemaphoreType.DMA
    results = (
        jax.ShapeDtypeStruct(whole, f32),
        jax.ShapeDtypeStruct(whole, f32),
        jax.ShapeDtypeStruct(whole, f32),
        jax.ShapeDtypeStruct(amax.shape, f32),
        jax.ShapeDtypeStruct(grouped, bf16),
    )
    outs = pl.pallas_call(
        functools.partial(fused_kernel, owners),
        out_shape=tuple(pltpu.VMEM(r.shape, r.dtype) for r in results),
        in_specs=[hbm] * 8 + [pl.BlockSpec(memory_space=pltpu.SMEM)],
        out_specs=(vmem,) * 5,
        scratch_shapes=(
            [pltpu.VMEM(whole, bf16)] * 6
            + [pltpu.VMEM(whole, f32)] * 3
            + [pltpu.VMEM(whole, bf16), pltpu.VMEM(grouped, bf16)]
            + [pltpu.VMEM((blocks, TILE, cols), bf16), pltpu.VMEM(grouped, bf16)]
            + [pltpu.SMEM(amax.shape, f32), pltpu.VMEM((1, TILE), jnp.int32)]
            + [
                dma((9,)), dma((n,)), dma((n,)), dma((blocks,)), dma((blocks,)), dma((n,)), dma((n,)),
                dma((n, owners - 1)), dma((n, owners - 1)),
            ]
        ),
        compiler_params=pltpu.CompilerParams(
            collective_id=0, has_side_effects=True, vmem_limit_bytes=32 * 1024 * 1024
        ),
    )(*[
        pltpu.with_memory_space_constraint(x, pltpu.HBM)
        for x in (
            gradients[0], master, one, two, synced, rollout.reshape(grouped), amax,
            table.reshape(1, TILE),
        )
    ], shifts)
    outs = pl.pallas_call(
        write_kernel,
        out_shape=results,
        in_specs=[vmem] * 5,
        out_specs=(hbm,) * 5,
        scratch_shapes=[dma((5,))],
        compiler_params=pltpu.CompilerParams(vmem_limit_bytes=4 * 1024 * 1024),
    )(*[pltpu.with_memory_space_constraint(x, pltpu.VMEM) for x in outs])
    return outs[0], outs[1], outs[2], outs[3], outs[4].reshape(whole)


def owner_rows(row_table, expert_owner, blocks, owner_count):
    per_owner = TILE // owner_count
    ordering = jnp.argsort(row_table, stable=True)
    experts = blocks * TILE // D
    shifts = expert_owner[experts]
    owners = jnp.arange(owner_count, dtype=jnp.int32)
    first_slot = (owners[None, :] - shifts[:, None]) % owner_count * per_owner
    return ordering[first_slot[:, :, None] + jnp.arange(per_owner, dtype=jnp.int32)[None, None, :]]


def plain_body(
    gradients, master, moment_one, moment_two, synced, rollout, amax_record, row_table, expert_owner
):
    owner_count = lax.axis_size("fsdp")
    replica_count = lax.axis_size("dp")
    row_count, column_count = master.shape
    summed = lax.psum_scatter(
        gradients[0].astype(jnp.float32).astype(jnp.bfloat16), "dp", scatter_dimension=1, tiled=True
    ).astype(jnp.float32)
    new_master, new_one, new_two = adam_step(master, moment_one, moment_two, summed / replica_count)
    difference = new_master - synced.astype(jnp.float32)
    block_count = row_count // TILE
    tile_count = column_count // TILE
    tiled_delta = difference.reshape(block_count, TILE, tile_count, TILE)
    new_amax = jnp.max(jnp.abs(tiled_delta), axis=(1, 3))
    scales = amax_record / code_limit
    code_values = (
        jnp.clip(tiled_delta / scales[:, None, :, None], -code_limit, code_limit)
        .astype(jnp.bfloat16)
        .reshape(block_count, TILE, column_count)
    )
    blocks = lax.axis_index("fsdp") * block_count + jnp.arange(block_count, dtype=jnp.int32)
    chosen = owner_rows(row_table, expert_owner, blocks, owner_count)
    per_owner = TILE // owner_count
    ordered = code_values[jnp.arange(block_count, dtype=jnp.int32)[:, None, None], chosen]
    outgoing = jnp.transpose(ordered, (1, 0, 2, 3)).reshape(
        owner_count, block_count * per_owner, column_count
    )
    spread = jnp.broadcast_to(scales[None], (owner_count, block_count, tile_count))
    incoming, scales_in = (
        lax.all_to_all(outgoing, "fsdp", split_axis=0, concat_axis=0, tiled=True),
        lax.all_to_all(
            spread.astype(jnp.bfloat16), "fsdp", split_axis=0, concat_axis=0, tiled=True
        ).astype(spread.dtype),
    )
    restored = (
        incoming.reshape(owner_count, block_count, per_owner, tile_count, TILE).astype(jnp.float32)
        * scales_in[:, :, None, :, None]
    )
    new_rollout = (rollout.astype(jnp.float32) + restored.reshape(row_count, column_count)).astype(
        jnp.bfloat16
    )
    return (new_master, new_one, new_two, new_amax, new_rollout)


def solution(mesh):
    sizes = dict(mesh.shape)
    fits = sizes["dp"] == 4 and sizes["fsdp"] == 8
    return jax.shard_map(
        fused_body if fits else plain_body,
        mesh=mesh,
        in_specs=(
            P("dp", "fsdp", None),
            P("fsdp", "dp"),
            P("fsdp", "dp"),
            P("fsdp", "dp"),
            P("fsdp", "dp"),
            P("fsdp", "dp"),
            P("fsdp", "dp"),
            P(),
            P(),
        ),
        out_specs=(
            P("fsdp", "dp"),
            P("fsdp", "dp"),
            P("fsdp", "dp"),
            P("fsdp", "dp"),
            P("fsdp", "dp"),
        ),
        check_vma=False,
    )
```

```python
import functools

import jax
import jax.numpy as jnp
from jax import lax
from jax.experimental import pallas as pl
from jax.experimental.pallas import tpu as pltpu
from jax.sharding import PartitionSpec as P

D = 7168
TILE = 128
MESH = pl.DeviceIdType.MESH

beta_one = 0.9
beta_two = 0.95
bias_one = 1.0 - 0.9**10
bias_two = 1.0 - 0.95**10
step_size = 0.05
weight_decay = 0.1
adam_floor = 1e-08
code_limit = 448.0


def adam_step(master, moment_one, moment_two, gradient):
    new_one = beta_one * moment_one + (1.0 - beta_one) * gradient
    new_two = beta_two * moment_two + (1.0 - beta_two) * gradient * gradient
    update = new_one / bias_one / (jnp.sqrt(new_two / bias_two) + adam_floor)
    new_master = master - step_size * (update + weight_decay * master)
    return (new_master, new_one, new_two)


SPLIT = 4


def flipped(index, mask):
    out = index
    bit = 1
    while bit <= mask:
        if mask & bit:
            out = out + bit - 2 * bit * (lax.rem(index // bit, 2))
        bit *= 2
    return out


def adam_fast(master, moment_one, moment_two, summed, replicas):
    new_one = beta_one * moment_one + ((1.0 - beta_one) / replicas) * summed
    new_two = beta_two * moment_two + ((1.0 - beta_two) / replicas**2) * (summed * summed)
    root = jnp.sqrt(new_two * (1.0 / bias_two)) + adam_floor
    new_master = (1.0 - step_size * weight_decay) * master - (step_size / bias_one) * new_one / root
    return (new_master, new_one, new_two)


def fused_kernel(
    owners, grads, master, one, two, synced, rollout, amax_h, table_h, shifts,
    master_w, one_w, two_w, amax_out, rollout_w,
    far_own, near_own, far_sib, near_sib, far_sum, far_in,
    master_v, one_v, two_v, synced_v, rollout_v, packed, arrived, amax, table, peaks,
    load_sem, far_send, far_recv, near_send, near_recv, x_send, x_recv, row_send, row_recv,
):
    d = lax.axis_index("dp")
    f = lax.axis_index("fsdp")
    rows, cols = master_v.shape
    blocks = rows // TILE
    width = cols // SPLIT
    part = TILE // owners
    chunks = [(b, h) for b in range(blocks) for h in range(SPLIT)]
    sib = flipped(d, 1)
    opp = flipped(d, 2)
    opp_sib = flipped(d, 3)

    barrier = pltpu.get_barrier_semaphore()
    pl.semaphore_signal(barrier, inc=1, device_id={"dp": sib}, device_id_type=MESH)
    pl.semaphore_signal(barrier, inc=1, device_id={"dp": opp}, device_id_type=MESH)
    for j in range(1, owners):
        pl.semaphore_signal(barrier, inc=1, device_id={"fsdp": flipped(f, j)}, device_id_type=MESH)

    def columns(q):
        return pl.ds(pl.multiple_of(q * cols, cols), cols)

    loads = [
        pltpu.make_async_copy(src, dst, load_sem.at[n])
        for n, (src, dst) in enumerate([
            (table_h, table),
            (amax_h, amax),
            (grads.at[:, columns(opp)], far_own),
            (grads.at[:, columns(d)], near_own),
            (one, one_v),
            (two, two_v),
            (master, master_v),
            (synced, synced_v),
            (rollout, rollout_v),
        ])
    ]
    for load in loads[:4]:
        load.start()

    def chooser(b):
        shift = shifts[((f * blocks + b) * TILE) // D]
        dest = (rank + shift * part) & (TILE - 1)
        return jnp.where(ti == dest, 1.0, 0.0).astype(jnp.bfloat16)

    pl.semaphore_wait(barrier, owners + 1)

    def at(ref, b, h):
        return ref.at[pl.ds(b * TILE, TILE), pl.ds(h * width, width)]

    far_copies = []
    for n, (b, h) in enumerate(chunks):
        source = pl.multiple_of(opp_sib * cols + h * width, width)
        copy = pltpu.make_async_remote_copy(
            src_ref=grads.at[pl.ds(b * TILE, TILE), pl.ds(source, width)],
            dst_ref=at(far_sib, b, h),
            send_sem=far_send.at[n], recv_sem=far_recv.at[n],
            device_id={"dp": sib}, device_id_type=MESH,
        )
        copy.start()
        far_copies.append(copy)
    near_copies = []
    for b in range(blocks):
        copy = pltpu.make_async_remote_copy(
            src_ref=grads.at[pl.ds(b * TILE, TILE), columns(sib)],
            dst_ref=near_sib.at[pl.ds(b * TILE, TILE), :],
            send_sem=near_send.at[b], recv_sem=near_recv.at[b],
            device_id={"dp": sib}, device_id_type=MESH,
        )
        copy.start()
        near_copies.append(copy)

    for load in loads[4:]:
        load.start()

    x_copies = []
    loads[2].wait()
    for n, (b, h) in enumerate(chunks):
        far_copies[n].wait_recv()
        mine = at(far_own, b, h)[...].astype(jnp.float32)
        theirs = at(far_sib, b, h)[...].astype(jnp.float32)
        at(far_sum, b, h)[...] = (mine + theirs).astype(jnp.bfloat16)
        copy = pltpu.make_async_remote_copy(
            src_ref=at(far_sum, b, h), dst_ref=at(far_in, b, h),
            send_sem=x_send.at[n], recv_sem=x_recv.at[n],
            device_id={"dp": opp}, device_id_type=MESH,
        )
        copy.start()
        x_copies.append(copy)

    for load in loads[:2]:
        load.wait()

    ti = lax.broadcasted_iota(jnp.int32, (TILE, TILE), 0)
    tj = lax.broadcasted_iota(jnp.int32, (TILE, TILE), 1)
    key_row = table[...] * TILE + lax.broadcasted_iota(jnp.int32, (1, TILE), 1)
    key_mat = jnp.broadcast_to(key_row, (TILE, TILE)).astype(jnp.float32)
    key_col = jnp.sum(jnp.where(ti == tj, key_mat, 0.0), axis=1, keepdims=True)
    rank = jnp.sum(jnp.where(key_col < key_mat, 1.0, 0.0), axis=0, keepdims=True).astype(jnp.int32)
    for load in loads[3:]:
        load.wait()

    targets = [flipped(f, j) for j in sorted(range(1, owners), key=lambda j: -(j // 2))]
    choose = None
    for n, (b, h) in enumerate(chunks):
        if h == 0:
            near_copies[b].wait_recv()
            choose = chooser(b)
        x_copies[n].wait_recv()
        summed = (
            at(near_own, b, h)[...].astype(jnp.float32)
            + at(near_sib, b, h)[...].astype(jnp.float32)
            + at(far_in, b, h)[...].astype(jnp.float32)
        )
        new_master, new_one, new_two = adam_fast(
            at(master_v, b, h)[...], at(one_v, b, h)[...], at(two_v, b, h)[...], summed, 4
        )
        at(master_w, b, h)[...] = new_master
        at(one_w, b, h)[...] = new_one
        at(two_w, b, h)[...] = new_two
        delta = new_master - at(synced_v, b, h)[...].astype(jnp.float32)
        restored = []
        for k in range(width // TILE):
            t = h * (width // TILE) + k
            piece = delta[:, k * TILE : (k + 1) * TILE]
            peaks[b, t] = jnp.max(jnp.abs(piece).reshape(TILE // 8, 8, TILE), axis=0)
            limit = amax[b, t] / code_limit * code_limit
            restored.append(jnp.clip(piece, -limit, limit).astype(jnp.bfloat16))
        restored = jnp.concatenate(restored, axis=1)
        packed[b, :, pl.ds(h * width, width)] = jnp.dot(
            choose, restored, preferred_element_type=jnp.float32
        ).astype(jnp.bfloat16)
        for target in targets:
            pltpu.make_async_remote_copy(
                src_ref=packed.at[b, pl.ds(pl.multiple_of(target * part, part), part), pl.ds(h * width, width)],
                dst_ref=arrived.at[f, b, :, pl.ds(h * width, width)],
                send_sem=row_send.at[n], recv_sem=row_recv.at[n],
                device_id={"fsdp": target}, device_id_type=MESH,
            ).start()
        arrived[f, b, :, pl.ds(h * width, width)] = packed[
            b, pl.ds(pl.multiple_of(f * part, part), part), pl.ds(h * width, width)
        ]

    for b in range(blocks):
        for t in range(cols // TILE):
            top = jnp.max(jnp.max(peaks[b, t], axis=0, keepdims=True), axis=1, keepdims=True)
            amax_out[b : b + 1, t : t + 1] = top

    for n, (b, h) in enumerate(chunks):
        cut = pl.ds(h * width, width)
        others = arrived.at[pl.ds(0, owners - 1), b, :, cut]
        pltpu.make_async_copy(others, others, row_recv.at[n]).wait()
        rollout_w[:, b, :, cut] = (
            rollout_v[:, b, :, cut].astype(jnp.float32) + arrived[:, b, :, cut].astype(jnp.float32)
        ).astype(jnp.bfloat16)

    for copy in far_copies + near_copies + x_copies:
        copy.wait_send()
    for n, (b, h) in enumerate(chunks):
        others = arrived.at[pl.ds(0, owners - 1), b, :, pl.ds(h * width, width)]
        pltpu.make_async_copy(others, others, row_send.at[n]).wait()


def write_kernel(*refs):
    count = len(refs) // 2
    sem = refs[-1]
    copies = [pltpu.make_async_copy(refs[n], refs[count + n], sem.at[n]) for n in range(count)]
    for copy in copies:
        copy.start()
    for copy in copies:
        copy.wait()


def fused_body(gradients, master, one, two, synced, rollout, amax, table, shifts):
    owners = lax.axis_size("fsdp")
    rows, cols = master.shape
    blocks = rows // TILE
    part = TILE // owners
    n = blocks * SPLIT
    f32, bf16 = jnp.float32, jnp.bfloat16
    hbm = pl.BlockSpec(memory_space=pltpu.HBM)
    vmem = pl.BlockSpec(memory_space=pltpu.VMEM)
    grouped = (owners, blocks, part, cols)
    whole = (rows, cols)
    dma = pltpu.SemaphoreType.DMA
    results = (
        jax.ShapeDtypeStruct(whole, f32),
        jax.ShapeDtypeStruct(whole, f32),
        jax.ShapeDtypeStruct(whole, f32),
        jax.ShapeDtypeStruct(amax.shape, f32),
        jax.ShapeDtypeStruct(grouped, bf16),
    )
    outs = pl.pallas_call(
        functools.partial(fused_kernel, owners),
        out_shape=tuple(pltpu.VMEM(r.shape, r.dtype) for r in results),
        in_specs=[hbm] * 8 + [pl.BlockSpec(memory_space=pltpu.SMEM)],
        out_specs=(vmem,) * 5,
        scratch_shapes=(
            [pltpu.VMEM(whole, bf16)] * 6
            + [pltpu.VMEM(whole, f32)] * 3
            + [pltpu.VMEM(whole, bf16), pltpu.VMEM(grouped, bf16)]
            + [pltpu.VMEM((blocks, TILE, cols), bf16), pltpu.VMEM(grouped, bf16)]
            + [pltpu.SMEM(amax.shape, f32), pltpu.VMEM((1, TILE), jnp.int32)]
            + [pltpu.VMEM((blocks, cols // TILE, 8, TILE), f32)]
            + [
                dma((9,)), dma((n,)), dma((n,)), dma((blocks,)), dma((blocks,)), dma((n,)), dma((n,)),
                dma((n,)), dma((n,)),
            ]
        ),
        compiler_params=pltpu.CompilerParams(
            collective_id=0, has_side_effects=True, vmem_limit_bytes=32 * 1024 * 1024
        ),
    )(*[
        pltpu.with_memory_space_constraint(x, pltpu.HBM)
        for x in (
            gradients[0], master, one, two, synced, rollout.reshape(grouped), amax,
            table.reshape(1, TILE),
        )
    ], shifts)
    outs = pl.pallas_call(
        write_kernel,
        out_shape=results,
        in_specs=[vmem] * 5,
        out_specs=(hbm,) * 5,
        scratch_shapes=[dma((5,))],
        compiler_params=pltpu.CompilerParams(vmem_limit_bytes=4 * 1024 * 1024),
    )(*[pltpu.with_memory_space_constraint(x, pltpu.VMEM) for x in outs])
    return outs[0], outs[1], outs[2], outs[3], outs[4].reshape(whole)


def owner_rows(row_table, expert_owner, blocks, owner_count):
    per_owner = TILE // owner_count
    ordering = jnp.argsort(row_table, stable=True)
    experts = blocks * TILE // D
    shifts = expert_owner[experts]
    owners = jnp.arange(owner_count, dtype=jnp.int32)
    first_slot = (owners[None, :] - shifts[:, None]) % owner_count * per_owner
    return ordering[first_slot[:, :, None] + jnp.arange(per_owner, dtype=jnp.int32)[None, None, :]]


def plain_body(
    gradients, master, moment_one, moment_two, synced, rollout, amax_record, row_table, expert_owner
):
    owner_count = lax.axis_size("fsdp")
    replica_count = lax.axis_size("dp")
    row_count, column_count = master.shape
    summed = lax.psum_scatter(
        gradients[0].astype(jnp.float32).astype(jnp.bfloat16), "dp", scatter_dimension=1, tiled=True
    ).astype(jnp.float32)
    new_master, new_one, new_two = adam_step(master, moment_one, moment_two, summed / replica_count)
    difference = new_master - synced.astype(jnp.float32)
    block_count = row_count // TILE
    tile_count = column_count // TILE
    tiled_delta = difference.reshape(block_count, TILE, tile_count, TILE)
    new_amax = jnp.max(jnp.abs(tiled_delta), axis=(1, 3))
    scales = amax_record / code_limit
    code_values = (
        jnp.clip(tiled_delta / scales[:, None, :, None], -code_limit, code_limit)
        .astype(jnp.bfloat16)
        .reshape(block_count, TILE, column_count)
    )
    blocks = lax.axis_index("fsdp") * block_count + jnp.arange(block_count, dtype=jnp.int32)
    chosen = owner_rows(row_table, expert_owner, blocks, owner_count)
    per_owner = TILE // owner_count
    ordered = code_values[jnp.arange(block_count, dtype=jnp.int32)[:, None, None], chosen]
    outgoing = jnp.transpose(ordered, (1, 0, 2, 3)).reshape(
        owner_count, block_count * per_owner, column_count
    )
    spread = jnp.broadcast_to(scales[None], (owner_count, block_count, tile_count))
    incoming, scales_in = (
        lax.all_to_all(outgoing, "fsdp", split_axis=0, concat_axis=0, tiled=True),
        lax.all_to_all(
            spread.astype(jnp.bfloat16), "fsdp", split_axis=0, concat_axis=0, tiled=True
        ).astype(spread.dtype),
    )
    restored = (
        incoming.reshape(owner_count, block_count, per_owner, tile_count, TILE).astype(jnp.float32)
        * scales_in[:, :, None, :, None]
    )
    new_rollout = (rollout.astype(jnp.float32) + restored.reshape(row_count, column_count)).astype(
        jnp.bfloat16
    )
    return (new_master, new_one, new_two, new_amax, new_rollout)


def solution(mesh):
    sizes = dict(mesh.shape)
    fits = sizes["dp"] == 4 and sizes["fsdp"] == 8
    return jax.shard_map(
        fused_body if fits else plain_body,
        mesh=mesh,
        in_specs=(
            P("dp", "fsdp", None),
            P("fsdp", "dp"),
            P("fsdp", "dp"),
            P("fsdp", "dp"),
            P("fsdp", "dp"),
            P("fsdp", "dp"),
            P("fsdp", "dp"),
            P(),
            P(),
        ),
        out_specs=(
            P("fsdp", "dp"),
            P("fsdp", "dp"),
            P("fsdp", "dp"),
            P("fsdp", "dp"),
            P("fsdp", "dp"),
        ),
        check_vma=False,
    )
```

```python
import functools

import jax
import jax.numpy as jnp
from jax import lax
from jax.experimental import pallas as pl
from jax.experimental.pallas import tpu as pltpu
from jax.sharding import PartitionSpec as P

D = 7168
TILE = 128
MESH = pl.DeviceIdType.MESH

beta_one = 0.9
beta_two = 0.95
bias_one = 1.0 - 0.9**10
bias_two = 1.0 - 0.95**10
step_size = 0.05
weight_decay = 0.1
adam_floor = 1e-08
code_limit = 448.0


def adam_step(master, moment_one, moment_two, gradient):
    new_one = beta_one * moment_one + (1.0 - beta_one) * gradient
    new_two = beta_two * moment_two + (1.0 - beta_two) * gradient * gradient
    update = new_one / bias_one / (jnp.sqrt(new_two / bias_two) + adam_floor)
    new_master = master - step_size * (update + weight_decay * master)
    return (new_master, new_one, new_two)


SPLIT = 4
WINDOW = 3


def flipped(index, mask):
    out = index
    bit = 1
    while bit <= mask:
        if mask & bit:
            out = out + bit - 2 * bit * (lax.rem(index // bit, 2))
        bit *= 2
    return out


def adam_fast(master, moment_one, moment_two, summed, replicas):
    new_one = beta_one * moment_one + ((1.0 - beta_one) / replicas) * summed
    new_two = beta_two * moment_two + ((1.0 - beta_two) / replicas**2) * (summed * summed)
    root = jnp.sqrt(new_two * (1.0 / bias_two)) + adam_floor
    new_master = (1.0 - step_size * weight_decay) * master - (step_size / bias_one) * new_one / root
    return (new_master, new_one, new_two)


def fused_kernel(
    owners, grads, master, one, two, synced, rollout, amax_h, table_h, shifts,
    master_w, one_w, two_w, amax_out, rollout_w,
    far_own, near_own, far_sib, near_sib, far_sum, far_in,
    master_v, one_v, two_v, synced_v, rollout_v, packed, arrived, amax, table, peaks,
    load_sem, far_send, far_recv, near_send, near_recv, x_send, x_recv, row_send, row_recv,
):
    d = lax.axis_index("dp")
    f = lax.axis_index("fsdp")
    rows, cols = master_v.shape
    blocks = rows // TILE
    width = cols // SPLIT
    part = TILE // owners
    chunks = [(b, h) for b in range(blocks) for h in range(SPLIT)]
    sib = flipped(d, 1)
    opp = flipped(d, 2)
    opp_sib = flipped(d, 3)

    barrier = pltpu.get_barrier_semaphore()
    pl.semaphore_signal(barrier, inc=1, device_id={"dp": sib}, device_id_type=MESH)
    pl.semaphore_signal(barrier, inc=1, device_id={"dp": opp}, device_id_type=MESH)
    for j in range(1, owners):
        pl.semaphore_signal(barrier, inc=1, device_id={"fsdp": flipped(f, j)}, device_id_type=MESH)

    def columns(q):
        return pl.ds(pl.multiple_of(q * cols, cols), cols)

    loads = [
        pltpu.make_async_copy(src, dst, load_sem.at[n])
        for n, (src, dst) in enumerate([
            (table_h, table),
            (amax_h, amax),
            (grads.at[:, columns(opp)], far_own),
            (grads.at[:, columns(d)], near_own),
            (one, one_v),
            (two, two_v),
            (master, master_v),
            (synced, synced_v),
            (rollout, rollout_v),
        ])
    ]
    for load in loads[:4]:
        load.start()

    def chooser(b):
        shift = shifts[((f * blocks + b) * TILE) // D]
        dest = (rank + shift * part) & (TILE - 1)
        return jnp.where(ti == dest, 1.0, 0.0).astype(jnp.bfloat16)

    pl.semaphore_wait(barrier, owners + 1)

    def at(ref, b, h):
        return ref.at[pl.ds(b * TILE, TILE), pl.ds(h * width, width)]

    far_copies = []
    for n, (b, h) in enumerate(chunks):
        source = pl.multiple_of(opp_sib * cols + h * width, width)
        copy = pltpu.make_async_remote_copy(
            src_ref=grads.at[pl.ds(b * TILE, TILE), pl.ds(source, width)],
            dst_ref=at(far_sib, b, h),
            send_sem=far_send.at[n], recv_sem=far_recv.at[n],
            device_id={"dp": sib}, device_id_type=MESH,
        )
        copy.start()
        far_copies.append(copy)
    near_copies = []
    for b in range(blocks):
        copy = pltpu.make_async_remote_copy(
            src_ref=grads.at[pl.ds(b * TILE, TILE), columns(sib)],
            dst_ref=near_sib.at[pl.ds(b * TILE, TILE), :],
            send_sem=near_send.at[b], recv_sem=near_recv.at[b],
            device_id={"dp": sib}, device_id_type=MESH,
        )
        copy.start()
        near_copies.append(copy)

    for load in loads[4:]:
        load.start(priority=1)

    x_copies = []
    loads[2].wait()

    def send_x(n):
        b, h = chunks[n]
        far_copies[n].wait_recv()
        mine = at(far_own, b, h)[...].astype(jnp.float32)
        theirs = at(far_sib, b, h)[...].astype(jnp.float32)
        at(far_sum, b, h)[...] = (mine + theirs).astype(jnp.bfloat16)
        copy = pltpu.make_async_remote_copy(
            src_ref=at(far_sum, b, h), dst_ref=at(far_in, b, h),
            send_sem=x_send.at[n], recv_sem=x_recv.at[n],
            device_id={"dp": opp}, device_id_type=MESH,
        )
        copy.start()
        x_copies.append(copy)

    for n in range(WINDOW):
        send_x(n)

    for load in loads[:2]:
        load.wait()

    ti = lax.broadcasted_iota(jnp.int32, (TILE, TILE), 0)
    tj = lax.broadcasted_iota(jnp.int32, (TILE, TILE), 1)
    key_row = table[...] * TILE + lax.broadcasted_iota(jnp.int32, (1, TILE), 1)
    key_mat = jnp.broadcast_to(key_row, (TILE, TILE)).astype(jnp.float32)
    key_col = jnp.sum(jnp.where(ti == tj, key_mat, 0.0), axis=1, keepdims=True)
    rank = jnp.sum(jnp.where(key_col < key_mat, 1.0, 0.0), axis=0, keepdims=True).astype(jnp.int32)
    for load in loads[3:]:
        load.wait()

    targets = [flipped(f, j) for j in sorted(range(1, owners), key=lambda j: -(j // 2))]
    choose = None
    for n, (b, h) in enumerate(chunks):
        if h == 0:
            near_copies[b].wait_recv()
            choose = chooser(b)
        if n + WINDOW < len(chunks):
            send_x(n + WINDOW)
        x_copies[n].wait_recv()
        summed = (
            at(near_own, b, h)[...].astype(jnp.float32)
            + at(near_sib, b, h)[...].astype(jnp.float32)
            + at(far_in, b, h)[...].astype(jnp.float32)
        )
        new_master, new_one, new_two = adam_fast(
            at(master_v, b, h)[...], at(one_v, b, h)[...], at(two_v, b, h)[...], summed, 4
        )
        at(master_w, b, h)[...] = new_master
        at(one_w, b, h)[...] = new_one
        at(two_w, b, h)[...] = new_two
        delta = new_master - at(synced_v, b, h)[...].astype(jnp.float32)
        restored = []
        for k in range(width // TILE):
            t = h * (width // TILE) + k
            piece = delta[:, k * TILE : (k + 1) * TILE]
            peaks[b, t] = jnp.max(jnp.abs(piece).reshape(TILE // 8, 8, TILE), axis=0)
            limit = amax[b, t] / code_limit * code_limit
            restored.append(jnp.clip(piece, -limit, limit).astype(jnp.bfloat16))
        restored = jnp.concatenate(restored, axis=1)
        packed[b, :, pl.ds(h * width, width)] = jnp.dot(
            choose, restored, preferred_element_type=jnp.float32
        ).astype(jnp.bfloat16)
        for target in targets:
            pltpu.make_async_remote_copy(
                src_ref=packed.at[b, pl.ds(pl.multiple_of(target * part, part), part), pl.ds(h * width, width)],
                dst_ref=arrived.at[f, b, :, pl.ds(h * width, width)],
                send_sem=row_send.at[n], recv_sem=row_recv.at[n],
                device_id={"fsdp": target}, device_id_type=MESH,
            ).start()
        arrived[f, b, :, pl.ds(h * width, width)] = packed[
            b, pl.ds(pl.multiple_of(f * part, part), part), pl.ds(h * width, width)
        ]

    for b in range(blocks):
        for t in range(cols // TILE):
            top = jnp.max(jnp.max(peaks[b, t], axis=0, keepdims=True), axis=1, keepdims=True)
            amax_out[b : b + 1, t : t + 1] = top

    for n, (b, h) in enumerate(chunks):
        cut = pl.ds(h * width, width)
        others = arrived.at[pl.ds(0, owners - 1), b, :, cut]
        pltpu.make_async_copy(others, others, row_recv.at[n]).wait()
        rollout_w[:, b, :, cut] = (
            rollout_v[:, b, :, cut].astype(jnp.float32) + arrived[:, b, :, cut].astype(jnp.float32)
        ).astype(jnp.bfloat16)

    for copy in far_copies + near_copies + x_copies:
        copy.wait_send()
    for n, (b, h) in enumerate(chunks):
        others = arrived.at[pl.ds(0, owners - 1), b, :, pl.ds(h * width, width)]
        pltpu.make_async_copy(others, others, row_send.at[n]).wait()


def write_kernel(*refs):
    count = len(refs) // 2
    sem = refs[-1]
    copies = [pltpu.make_async_copy(refs[n], refs[count + n], sem.at[n]) for n in range(count)]
    for copy in copies:
        copy.start()
    for copy in copies:
        copy.wait()


def fused_body(gradients, master, one, two, synced, rollout, amax, table, shifts):
    owners = lax.axis_size("fsdp")
    rows, cols = master.shape
    blocks = rows // TILE
    part = TILE // owners
    n = blocks * SPLIT
    f32, bf16 = jnp.float32, jnp.bfloat16
    hbm = pl.BlockSpec(memory_space=pltpu.HBM)
    vmem = pl.BlockSpec(memory_space=pltpu.VMEM)
    grouped = (owners, blocks, part, cols)
    whole = (rows, cols)
    dma = pltpu.SemaphoreType.DMA
    results = (
        jax.ShapeDtypeStruct(whole, f32),
        jax.ShapeDtypeStruct(whole, f32),
        jax.ShapeDtypeStruct(whole, f32),
        jax.ShapeDtypeStruct(amax.shape, f32),
        jax.ShapeDtypeStruct(grouped, bf16),
    )
    outs = pl.pallas_call(
        functools.partial(fused_kernel, owners),
        out_shape=tuple(pltpu.VMEM(r.shape, r.dtype) for r in results),
        in_specs=[hbm] * 8 + [pl.BlockSpec(memory_space=pltpu.SMEM)],
        out_specs=(vmem,) * 5,
        scratch_shapes=(
            [pltpu.VMEM(whole, bf16)] * 6
            + [pltpu.VMEM(whole, f32)] * 3
            + [pltpu.VMEM(whole, bf16), pltpu.VMEM(grouped, bf16)]
            + [pltpu.VMEM((blocks, TILE, cols), bf16), pltpu.VMEM(grouped, bf16)]
            + [pltpu.SMEM(amax.shape, f32), pltpu.VMEM((1, TILE), jnp.int32)]
            + [pltpu.VMEM((blocks, cols // TILE, 8, TILE), f32)]
            + [
                dma((9,)), dma((n,)), dma((n,)), dma((blocks,)), dma((blocks,)), dma((n,)), dma((n,)),
                dma((n,)), dma((n,)),
            ]
        ),
        compiler_params=pltpu.CompilerParams(
            collective_id=0, has_side_effects=True, vmem_limit_bytes=32 * 1024 * 1024
        ),
    )(*[
        pltpu.with_memory_space_constraint(x, pltpu.HBM)
        for x in (
            gradients[0], master, one, two, synced, rollout.reshape(grouped), amax,
            table.reshape(1, TILE),
        )
    ], shifts)
    outs = pl.pallas_call(
        write_kernel,
        out_shape=results,
        in_specs=[vmem] * 5,
        out_specs=(hbm,) * 5,
        scratch_shapes=[dma((5,))],
        compiler_params=pltpu.CompilerParams(vmem_limit_bytes=4 * 1024 * 1024),
    )(*[pltpu.with_memory_space_constraint(x, pltpu.VMEM) for x in outs])
    return outs[0], outs[1], outs[2], outs[3], outs[4].reshape(whole)


def owner_rows(row_table, expert_owner, blocks, owner_count):
    per_owner = TILE // owner_count
    ordering = jnp.argsort(row_table, stable=True)
    experts = blocks * TILE // D
    shifts = expert_owner[experts]
    owners = jnp.arange(owner_count, dtype=jnp.int32)
    first_slot = (owners[None, :] - shifts[:, None]) % owner_count * per_owner
    return ordering[first_slot[:, :, None] + jnp.arange(per_owner, dtype=jnp.int32)[None, None, :]]


def plain_body(
    gradients, master, moment_one, moment_two, synced, rollout, amax_record, row_table, expert_owner
):
    owner_count = lax.axis_size("fsdp")
    replica_count = lax.axis_size("dp")
    row_count, column_count = master.shape
    summed = lax.psum_scatter(
        gradients[0].astype(jnp.float32).astype(jnp.bfloat16), "dp", scatter_dimension=1, tiled=True
    ).astype(jnp.float32)
    new_master, new_one, new_two = adam_step(master, moment_one, moment_two, summed / replica_count)
    difference = new_master - synced.astype(jnp.float32)
    block_count = row_count // TILE
    tile_count = column_count // TILE
    tiled_delta = difference.reshape(block_count, TILE, tile_count, TILE)
    new_amax = jnp.max(jnp.abs(tiled_delta), axis=(1, 3))
    scales = amax_record / code_limit
    code_values = (
        jnp.clip(tiled_delta / scales[:, None, :, None], -code_limit, code_limit)
        .astype(jnp.bfloat16)
        .reshape(block_count, TILE, column_count)
    )
    blocks = lax.axis_index("fsdp") * block_count + jnp.arange(block_count, dtype=jnp.int32)
    chosen = owner_rows(row_table, expert_owner, blocks, owner_count)
    per_owner = TILE // owner_count
    ordered = code_values[jnp.arange(block_count, dtype=jnp.int32)[:, None, None], chosen]
    outgoing = jnp.transpose(ordered, (1, 0, 2, 3)).reshape(
        owner_count, block_count * per_owner, column_count
    )
    spread = jnp.broadcast_to(scales[None], (owner_count, block_count, tile_count))
    incoming, scales_in = (
        lax.all_to_all(outgoing, "fsdp", split_axis=0, concat_axis=0, tiled=True),
        lax.all_to_all(
            spread.astype(jnp.bfloat16), "fsdp", split_axis=0, concat_axis=0, tiled=True
        ).astype(spread.dtype),
    )
    restored = (
        incoming.reshape(owner_count, block_count, per_owner, tile_count, TILE).astype(jnp.float32)
        * scales_in[:, :, None, :, None]
    )
    new_rollout = (rollout.astype(jnp.float32) + restored.reshape(row_count, column_count)).astype(
        jnp.bfloat16
    )
    return (new_master, new_one, new_two, new_amax, new_rollout)


def solution(mesh):
    sizes = dict(mesh.shape)
    fits = sizes["dp"] == 4 and sizes["fsdp"] == 8
    return jax.shard_map(
        fused_body if fits else plain_body,
        mesh=mesh,
        in_specs=(
            P("dp", "fsdp", None),
            P("fsdp", "dp"),
            P("fsdp", "dp"),
            P("fsdp", "dp"),
            P("fsdp", "dp"),
            P("fsdp", "dp"),
            P("fsdp", "dp"),
            P(),
            P(),
        ),
        out_specs=(
            P("fsdp", "dp"),
            P("fsdp", "dp"),
            P("fsdp", "dp"),
            P("fsdp", "dp"),
            P("fsdp", "dp"),
        ),
        check_vma=False,
    )
```

```python
import functools

import jax
import jax.numpy as jnp
from jax import lax
from jax.experimental import pallas as pl
from jax.experimental.pallas import tpu as pltpu
from jax.sharding import PartitionSpec as P

D = 7168
TILE = 128
MESH = pl.DeviceIdType.MESH

beta_one = 0.9
beta_two = 0.95
bias_one = 1.0 - 0.9**10
bias_two = 1.0 - 0.95**10
step_size = 0.05
weight_decay = 0.1
adam_floor = 1e-08
code_limit = 448.0


def adam_step(master, moment_one, moment_two, gradient):
    new_one = beta_one * moment_one + (1.0 - beta_one) * gradient
    new_two = beta_two * moment_two + (1.0 - beta_two) * gradient * gradient
    update = new_one / bias_one / (jnp.sqrt(new_two / bias_two) + adam_floor)
    new_master = master - step_size * (update + weight_decay * master)
    return (new_master, new_one, new_two)


SPLIT = 2


def flipped(index, mask):
    out = index
    bit = 1
    while bit <= mask:
        if mask & bit:
            out = out + bit - 2 * bit * (lax.rem(index // bit, 2))
        bit *= 2
    return out


def adam_fast(master, moment_one, moment_two, summed, replicas):
    new_one = beta_one * moment_one + ((1.0 - beta_one) / replicas) * summed
    new_two = beta_two * moment_two + ((1.0 - beta_two) / replicas**2) * (summed * summed)
    root = jnp.sqrt(new_two * (1.0 / bias_two)) + adam_floor
    new_master = (1.0 - step_size * weight_decay) * master - (step_size / bias_one) * new_one / root
    return (new_master, new_one, new_two)


def fused_kernel(
    owners, grads, master, one, two, synced, rollout, amax_h, table_h, shifts,
    master_w, one_w, two_w, amax_out, rollout_w,
    far_own, near_own, far_sib, near_sib, far_sum, far_in,
    master_v, one_v, two_v, synced_v, rollout_v, packed, arrived, amax, table, peaks,
    load_sem, far_send, far_recv, near_send, near_recv, x_send, x_recv, row_send, row_recv,
):
    d = lax.axis_index("dp")
    f = lax.axis_index("fsdp")
    rows, cols = master_v.shape
    blocks = rows // TILE
    width = cols // SPLIT
    part = TILE // owners
    chunks = [(b, h) for b in range(blocks) for h in range(SPLIT)]
    sib = flipped(d, 1)
    opp = flipped(d, 2)
    opp_sib = flipped(d, 3)

    barrier = pltpu.get_barrier_semaphore()
    pl.semaphore_signal(barrier, inc=1, device_id={"dp": sib}, device_id_type=MESH)
    pl.semaphore_signal(barrier, inc=1, device_id={"dp": opp}, device_id_type=MESH)
    for j in range(1, owners):
        pl.semaphore_signal(barrier, inc=1, device_id={"fsdp": flipped(f, j)}, device_id_type=MESH)

    def columns(q):
        return pl.ds(pl.multiple_of(q * cols, cols), cols)

    loads = [
        pltpu.make_async_copy(src, dst, load_sem.at[n])
        for n, (src, dst) in enumerate([
            (table_h, table),
            (amax_h, amax),
            (grads.at[:, columns(opp)], far_own),
            (grads.at[:, columns(d)], near_own),
            (one, one_v),
            (two, two_v),
            (master, master_v),
            (synced, synced_v),
            (rollout, rollout_v),
        ])
    ]
    for load in loads[:4]:
        load.start()

    def chooser(b):
        shift = shifts[((f * blocks + b) * TILE) // D]
        dest = (rank + shift * part) & (TILE - 1)
        return jnp.where(ti == dest, 1.0, 0.0).astype(jnp.bfloat16)

    pl.semaphore_wait(barrier, owners + 1)

    def at(ref, b, h):
        return ref.at[pl.ds(b * TILE, TILE), pl.ds(h * width, width)]

    far_copies = []
    for n, (b, h) in enumerate(chunks):
        source = pl.multiple_of(opp_sib * cols + h * width, width)
        copy = pltpu.make_async_remote_copy(
            src_ref=grads.at[pl.ds(b * TILE, TILE), pl.ds(source, width)],
            dst_ref=at(far_sib, b, h),
            send_sem=far_send.at[n], recv_sem=far_recv.at[n],
            device_id={"dp": sib}, device_id_type=MESH,
        )
        copy.start()
        far_copies.append(copy)
    near_copies = []
    for b in range(blocks):
        copy = pltpu.make_async_remote_copy(
            src_ref=grads.at[pl.ds(b * TILE, TILE), columns(sib)],
            dst_ref=near_sib.at[pl.ds(b * TILE, TILE), :],
            send_sem=near_send.at[b], recv_sem=near_recv.at[b],
            device_id={"dp": sib}, device_id_type=MESH,
        )
        copy.start()
        near_copies.append(copy)

    for load in loads[4:]:
        load.start()

    x_copies = []
    loads[2].wait()
    for n, (b, h) in enumerate(chunks):
        far_copies[n].wait_recv()
        mine = at(far_own, b, h)[...].astype(jnp.float32)
        theirs = at(far_sib, b, h)[...].astype(jnp.float32)
        at(far_sum, b, h)[...] = (mine + theirs).astype(jnp.bfloat16)
        copy = pltpu.make_async_remote_copy(
            src_ref=at(far_sum, b, h), dst_ref=at(far_in, b, h),
            send_sem=x_send.at[n], recv_sem=x_recv.at[n],
            device_id={"dp": opp}, device_id_type=MESH,
        )
        copy.start()
        x_copies.append(copy)

    for load in loads[:2]:
        load.wait()

    ti = lax.broadcasted_iota(jnp.int32, (TILE, TILE), 0)
    tj = lax.broadcasted_iota(jnp.int32, (TILE, TILE), 1)
    key_row = table[...] * TILE + lax.broadcasted_iota(jnp.int32, (1, TILE), 1)
    key_mat = jnp.broadcast_to(key_row, (TILE, TILE)).astype(jnp.float32)
    key_col = jnp.sum(jnp.where(ti == tj, key_mat, 0.0), axis=1, keepdims=True)
    rank = jnp.sum(jnp.where(key_col < key_mat, 1.0, 0.0), axis=0, keepdims=True).astype(jnp.int32)
    for load in loads[3:]:
        load.wait()

    targets = [flipped(f, j) for j in sorted(range(1, owners), key=lambda j: -(j // 2))]
    choose = None
    for n, (b, h) in enumerate(chunks):
        if h == 0:
            near_copies[b].wait_recv()
            choose = chooser(b)
        x_copies[n].wait_recv()
        summed = (
            at(near_own, b, h)[...].astype(jnp.float32)
            + at(near_sib, b, h)[...].astype(jnp.float32)
            + at(far_in, b, h)[...].astype(jnp.float32)
        )
        new_master, new_one, new_two = adam_fast(
            at(master_v, b, h)[...], at(one_v, b, h)[...], at(two_v, b, h)[...], summed, 4
        )
        at(master_w, b, h)[...] = new_master
        at(one_w, b, h)[...] = new_one
        at(two_w, b, h)[...] = new_two
        delta = new_master - at(synced_v, b, h)[...].astype(jnp.float32)
        restored = []
        for k in range(width // TILE):
            t = h * (width // TILE) + k
            piece = delta[:, k * TILE : (k + 1) * TILE]
            peaks[b, t] = jnp.max(jnp.abs(piece).reshape(TILE // 8, 8, TILE), axis=0)
            limit = amax[b, t] / code_limit * code_limit
            restored.append(jnp.clip(piece, -limit, limit).astype(jnp.bfloat16))
        restored = jnp.concatenate(restored, axis=1)
        packed[b, :, pl.ds(h * width, width)] = jnp.dot(
            choose, restored, preferred_element_type=jnp.float32
        ).astype(jnp.bfloat16)
        for target in targets:
            pltpu.make_async_remote_copy(
                src_ref=packed.at[b, pl.ds(pl.multiple_of(target * part, part), part), pl.ds(h * width, width)],
                dst_ref=arrived.at[f, b, :, pl.ds(h * width, width)],
                send_sem=row_send.at[n], recv_sem=row_recv.at[n],
                device_id={"fsdp": target}, device_id_type=MESH,
            ).start()
        arrived[f, b, :, pl.ds(h * width, width)] = packed[
            b, pl.ds(pl.multiple_of(f * part, part), part), pl.ds(h * width, width)
        ]

    for b in range(blocks):
        for t in range(cols // TILE):
            top = jnp.max(jnp.max(peaks[b, t], axis=0, keepdims=True), axis=1, keepdims=True)
            amax_out[b : b + 1, t : t + 1] = top

    for n, (b, h) in enumerate(chunks):
        cut = pl.ds(h * width, width)
        others = arrived.at[pl.ds(0, owners - 1), b, :, cut]
        pltpu.make_async_copy(others, others, row_recv.at[n]).wait()
        rollout_w[:, b, :, cut] = (
            rollout_v[:, b, :, cut].astype(jnp.float32) + arrived[:, b, :, cut].astype(jnp.float32)
        ).astype(jnp.bfloat16)

    for copy in far_copies + near_copies + x_copies:
        copy.wait_send()
    for n, (b, h) in enumerate(chunks):
        others = arrived.at[pl.ds(0, owners - 1), b, :, pl.ds(h * width, width)]
        pltpu.make_async_copy(others, others, row_send.at[n]).wait()


def write_kernel(*refs):
    count = len(refs) // 2
    sem = refs[-1]
    copies = [pltpu.make_async_copy(refs[n], refs[count + n], sem.at[n]) for n in range(count)]
    for copy in copies:
        copy.start()
    for copy in copies:
        copy.wait()


def fused_body(gradients, master, one, two, synced, rollout, amax, table, shifts):
    owners = lax.axis_size("fsdp")
    rows, cols = master.shape
    blocks = rows // TILE
    part = TILE // owners
    n = blocks * SPLIT
    f32, bf16 = jnp.float32, jnp.bfloat16
    hbm = pl.BlockSpec(memory_space=pltpu.HBM)
    vmem = pl.BlockSpec(memory_space=pltpu.VMEM)
    grouped = (owners, blocks, part, cols)
    whole = (rows, cols)
    dma = pltpu.SemaphoreType.DMA
    results = (
        jax.ShapeDtypeStruct(whole, f32),
        jax.ShapeDtypeStruct(whole, f32),
        jax.ShapeDtypeStruct(whole, f32),
        jax.ShapeDtypeStruct(amax.shape, f32),
        jax.ShapeDtypeStruct(grouped, bf16),
    )
    outs = pl.pallas_call(
        functools.partial(fused_kernel, owners),
        out_shape=tuple(pltpu.VMEM(r.shape, r.dtype) for r in results),
        in_specs=[hbm] * 8 + [pl.BlockSpec(memory_space=pltpu.SMEM)],
        out_specs=(vmem,) * 5,
        scratch_shapes=(
            [pltpu.VMEM(whole, bf16)] * 6
            + [pltpu.VMEM(whole, f32)] * 3
            + [pltpu.VMEM(whole, bf16), pltpu.VMEM(grouped, bf16)]
            + [pltpu.VMEM((blocks, TILE, cols), bf16), pltpu.VMEM(grouped, bf16)]
            + [pltpu.SMEM(amax.shape, f32), pltpu.VMEM((1, TILE), jnp.int32)]
            + [pltpu.VMEM((blocks, cols // TILE, 8, TILE), f32)]
            + [
                dma((9,)), dma((n,)), dma((n,)), dma((blocks,)), dma((blocks,)), dma((n,)), dma((n,)),
                dma((n,)), dma((n,)),
            ]
        ),
        compiler_params=pltpu.CompilerParams(
            collective_id=0, has_side_effects=True, vmem_limit_bytes=32 * 1024 * 1024
        ),
    )(*[
        pltpu.with_memory_space_constraint(x, pltpu.HBM)
        for x in (
            gradients[0], master, one, two, synced, rollout.reshape(grouped), amax,
            table.reshape(1, TILE),
        )
    ], shifts)
    outs = pl.pallas_call(
        write_kernel,
        out_shape=results,
        in_specs=[vmem] * 5,
        out_specs=(hbm,) * 5,
        scratch_shapes=[dma((5,))],
        compiler_params=pltpu.CompilerParams(vmem_limit_bytes=4 * 1024 * 1024),
    )(*[pltpu.with_memory_space_constraint(x, pltpu.VMEM) for x in outs])
    return outs[0], outs[1], outs[2], outs[3], outs[4].reshape(whole)


def owner_rows(row_table, expert_owner, blocks, owner_count):
    per_owner = TILE // owner_count
    ordering = jnp.argsort(row_table, stable=True)
    experts = blocks * TILE // D
    shifts = expert_owner[experts]
    owners = jnp.arange(owner_count, dtype=jnp.int32)
    first_slot = (owners[None, :] - shifts[:, None]) % owner_count * per_owner
    return ordering[first_slot[:, :, None] + jnp.arange(per_owner, dtype=jnp.int32)[None, None, :]]


def plain_body(
    gradients, master, moment_one, moment_two, synced, rollout, amax_record, row_table, expert_owner
):
    owner_count = lax.axis_size("fsdp")
    replica_count = lax.axis_size("dp")
    row_count, column_count = master.shape
    summed = lax.psum_scatter(
        gradients[0].astype(jnp.float32).astype(jnp.bfloat16), "dp", scatter_dimension=1, tiled=True
    ).astype(jnp.float32)
    new_master, new_one, new_two = adam_step(master, moment_one, moment_two, summed / replica_count)
    difference = new_master - synced.astype(jnp.float32)
    block_count = row_count // TILE
    tile_count = column_count // TILE
    tiled_delta = difference.reshape(block_count, TILE, tile_count, TILE)
    new_amax = jnp.max(jnp.abs(tiled_delta), axis=(1, 3))
    scales = amax_record / code_limit
    code_values = (
        jnp.clip(tiled_delta / scales[:, None, :, None], -code_limit, code_limit)
        .astype(jnp.bfloat16)
        .reshape(block_count, TILE, column_count)
    )
    blocks = lax.axis_index("fsdp") * block_count + jnp.arange(block_count, dtype=jnp.int32)
    chosen = owner_rows(row_table, expert_owner, blocks, owner_count)
    per_owner = TILE // owner_count
    ordered = code_values[jnp.arange(block_count, dtype=jnp.int32)[:, None, None], chosen]
    outgoing = jnp.transpose(ordered, (1, 0, 2, 3)).reshape(
        owner_count, block_count * per_owner, column_count
    )
    spread = jnp.broadcast_to(scales[None], (owner_count, block_count, tile_count))
    incoming, scales_in = (
        lax.all_to_all(outgoing, "fsdp", split_axis=0, concat_axis=0, tiled=True),
        lax.all_to_all(
            spread.astype(jnp.bfloat16), "fsdp", split_axis=0, concat_axis=0, tiled=True
        ).astype(spread.dtype),
    )
    restored = (
        incoming.reshape(owner_count, block_count, per_owner, tile_count, TILE).astype(jnp.float32)
        * scales_in[:, :, None, :, None]
    )
    new_rollout = (rollout.astype(jnp.float32) + restored.reshape(row_count, column_count)).astype(
        jnp.bfloat16
    )
    return (new_master, new_one, new_two, new_amax, new_rollout)


def solution(mesh):
    sizes = dict(mesh.shape)
    fits = sizes["dp"] == 4 and sizes["fsdp"] == 8
    return jax.shard_map(
        fused_body if fits else plain_body,
        mesh=mesh,
        in_specs=(
            P("dp", "fsdp", None),
            P("fsdp", "dp"),
            P("fsdp", "dp"),
            P("fsdp", "dp"),
            P("fsdp", "dp"),
            P("fsdp", "dp"),
            P("fsdp", "dp"),
            P(),
            P(),
        ),
        out_specs=(
            P("fsdp", "dp"),
            P("fsdp", "dp"),
            P("fsdp", "dp"),
            P("fsdp", "dp"),
            P("fsdp", "dp"),
        ),
        check_vma=False,
    )
```

```python
import functools

import jax
import jax.numpy as jnp
from jax import lax
from jax.experimental import pallas as pl
from jax.experimental.pallas import tpu as pltpu
from jax.sharding import PartitionSpec as P

D = 7168
TILE = 128
MESH = pl.DeviceIdType.MESH

beta_one = 0.9
beta_two = 0.95
bias_one = 1.0 - 0.9**10
bias_two = 1.0 - 0.95**10
step_size = 0.05
weight_decay = 0.1
adam_floor = 1e-08
code_limit = 448.0


def adam_step(master, moment_one, moment_two, gradient):
    new_one = beta_one * moment_one + (1.0 - beta_one) * gradient
    new_two = beta_two * moment_two + (1.0 - beta_two) * gradient * gradient
    update = new_one / bias_one / (jnp.sqrt(new_two / bias_two) + adam_floor)
    new_master = master - step_size * (update + weight_decay * master)
    return (new_master, new_one, new_two)


def chunks_of(blocks, cols):
    out = []
    for b in range(blocks):
        thin = cols // 2 if cols // 2 % TILE == 0 else cols
        widths = [thin] * (cols // thin)
        if thin % (2 * TILE) == 0:
            if b == 0:
                widths[:1] = [thin // 2] * 2
            if b == blocks - 1:
                widths[-1:] = [thin // 2] * 2
        start = 0
        for width in widths:
            out.append((b, start, width))
            start += width
    return out


def flipped(index, mask):
    out = index
    bit = 1
    while bit <= mask:
        if mask & bit:
            out = out + bit - 2 * bit * (lax.rem(index // bit, 2))
        bit *= 2
    return out


def adam_fast(master, moment_one, moment_two, summed, replicas):
    new_one = beta_one * moment_one + ((1.0 - beta_one) / replicas) * summed
    new_two = beta_two * moment_two + ((1.0 - beta_two) / replicas**2) * (summed * summed)
    root = jnp.sqrt(new_two * (1.0 / bias_two)) + adam_floor
    new_master = (1.0 - step_size * weight_decay) * master - (step_size / bias_one) * new_one / root
    return (new_master, new_one, new_two)


def fused_kernel(
    owners, grads, master, one, two, synced, rollout, amax_h, table_h, shifts,
    master_w, one_w, two_w, amax_out, rollout_w,
    far_own, near_own, far_sib, near_sib, far_sum, far_in,
    master_v, one_v, two_v, synced_v, rollout_v, packed, arrived, amax, table, peaks,
    load_sem, far_send, far_recv, near_send, near_recv, x_send, x_recv, row_send, row_recv,
):
    d = lax.axis_index("dp")
    f = lax.axis_index("fsdp")
    rows, cols = master_v.shape
    blocks = rows // TILE
    part = TILE // owners
    chunks = chunks_of(blocks, cols)
    sib = flipped(d, 1)
    opp = flipped(d, 2)
    opp_sib = flipped(d, 3)

    barrier = pltpu.get_barrier_semaphore()
    pl.semaphore_signal(barrier, inc=1, device_id={"dp": sib}, device_id_type=MESH)
    pl.semaphore_signal(barrier, inc=1, device_id={"dp": opp}, device_id_type=MESH)
    for j in range(1, owners):
        pl.semaphore_signal(barrier, inc=1, device_id={"fsdp": flipped(f, j)}, device_id_type=MESH)

    def columns(q):
        return pl.ds(pl.multiple_of(q * cols, cols), cols)

    loads = [
        pltpu.make_async_copy(src, dst, load_sem.at[n])
        for n, (src, dst) in enumerate([
            (table_h, table),
            (amax_h, amax),
            (grads.at[:, columns(opp)], far_own),
            (grads.at[:, columns(d)], near_own),
            (one, one_v),
            (two, two_v),
            (master, master_v),
            (synced, synced_v),
            (rollout, rollout_v),
        ])
    ]
    for load in loads[:4]:
        load.start()

    def chooser(b):
        shift = shifts[((f * blocks + b) * TILE) // D]
        dest = (rank + shift * part) & (TILE - 1)
        return jnp.where(ti == dest, 1.0, 0.0).astype(jnp.bfloat16)

    pl.semaphore_wait(barrier, owners + 1)

    def at(ref, b, c, width):
        return ref.at[pl.ds(b * TILE, TILE), pl.ds(c, width)]

    far_copies = []
    for n, (b, c, width) in enumerate(chunks):
        source = pl.multiple_of(opp_sib * cols + c, TILE)
        copy = pltpu.make_async_remote_copy(
            src_ref=grads.at[pl.ds(b * TILE, TILE), pl.ds(source, width)],
            dst_ref=at(far_sib, b, c, width),
            send_sem=far_send.at[n], recv_sem=far_recv.at[n],
            device_id={"dp": sib}, device_id_type=MESH,
        )
        copy.start()
        far_copies.append(copy)
    near_copies = []
    for b in range(blocks):
        copy = pltpu.make_async_remote_copy(
            src_ref=grads.at[pl.ds(b * TILE, TILE), columns(sib)],
            dst_ref=near_sib.at[pl.ds(b * TILE, TILE), :],
            send_sem=near_send.at[b], recv_sem=near_recv.at[b],
            device_id={"dp": sib}, device_id_type=MESH,
        )
        copy.start()
        near_copies.append(copy)

    for load in loads[4:]:
        load.start()

    x_copies = []
    loads[2].wait()
    for n, (b, c, width) in enumerate(chunks):
        far_copies[n].wait_recv()
        mine = at(far_own, b, c, width)[...].astype(jnp.float32)
        theirs = at(far_sib, b, c, width)[...].astype(jnp.float32)
        at(far_sum, b, c, width)[...] = (mine + theirs).astype(jnp.bfloat16)
        copy = pltpu.make_async_remote_copy(
            src_ref=at(far_sum, b, c, width), dst_ref=at(far_in, b, c, width),
            send_sem=x_send.at[n], recv_sem=x_recv.at[n],
            device_id={"dp": opp}, device_id_type=MESH,
        )
        copy.start()
        x_copies.append(copy)

    for load in loads[:2]:
        load.wait()

    ti = lax.broadcasted_iota(jnp.int32, (TILE, TILE), 0)
    tj = lax.broadcasted_iota(jnp.int32, (TILE, TILE), 1)
    key_row = table[...] * TILE + lax.broadcasted_iota(jnp.int32, (1, TILE), 1)
    key_mat = jnp.broadcast_to(key_row, (TILE, TILE)).astype(jnp.float32)
    key_col = jnp.sum(jnp.where(ti == tj, key_mat, 0.0), axis=1, keepdims=True)
    rank = jnp.sum(jnp.where(key_col < key_mat, 1.0, 0.0), axis=0, keepdims=True).astype(jnp.int32)
    for load in loads[3:]:
        load.wait()

    targets = [flipped(f, j) for j in sorted(range(1, owners), key=lambda j: -(j // 2))]
    choose = None
    for n, (b, c, width) in enumerate(chunks):
        if c == 0:
            near_copies[b].wait_recv()
            choose = chooser(b)
        x_copies[n].wait_recv()
        summed = (
            at(near_own, b, c, width)[...].astype(jnp.float32)
            + at(near_sib, b, c, width)[...].astype(jnp.float32)
            + at(far_in, b, c, width)[...].astype(jnp.float32)
        )
        new_master, new_one, new_two = adam_fast(
            at(master_v, b, c, width)[...], at(one_v, b, c, width)[...], at(two_v, b, c, width)[...], summed, 4
        )
        at(master_w, b, c, width)[...] = new_master
        at(one_w, b, c, width)[...] = new_one
        at(two_w, b, c, width)[...] = new_two
        delta = new_master - at(synced_v, b, c, width)[...].astype(jnp.float32)
        restored = []
        for k in range(width // TILE):
            t = c // TILE + k
            piece = delta[:, k * TILE : (k + 1) * TILE]
            peaks[b, t] = jnp.max(jnp.abs(piece).reshape(TILE // 8, 8, TILE), axis=0)
            limit = amax[b, t] / code_limit * code_limit
            restored.append(jnp.clip(piece, -limit, limit).astype(jnp.bfloat16))
        restored = jnp.concatenate(restored, axis=1)
        packed[b, :, pl.ds(c, width)] = jnp.dot(
            choose, restored, preferred_element_type=jnp.float32
        ).astype(jnp.bfloat16)
        for target in targets:
            pltpu.make_async_remote_copy(
                src_ref=packed.at[b, pl.ds(pl.multiple_of(target * part, part), part), pl.ds(c, width)],
                dst_ref=arrived.at[f, b, :, pl.ds(c, width)],
                send_sem=row_send.at[n], recv_sem=row_recv.at[n],
                device_id={"fsdp": target}, device_id_type=MESH,
            ).start()
        arrived[f, b, :, pl.ds(c, width)] = packed[
            b, pl.ds(pl.multiple_of(f * part, part), part), pl.ds(c, width)
        ]

    for b in range(blocks):
        for t in range(cols // TILE):
            top = jnp.max(jnp.max(peaks[b, t], axis=0, keepdims=True), axis=1, keepdims=True)
            amax_out[b : b + 1, t : t + 1] = top

    for n, (b, c, width) in enumerate(chunks):
        cut = pl.ds(c, width)
        others = arrived.at[pl.ds(0, owners - 1), b, :, cut]
        pltpu.make_async_copy(others, others, row_recv.at[n]).wait()
        rollout_w[:, b, :, cut] = (
            rollout_v[:, b, :, cut].astype(jnp.float32) + arrived[:, b, :, cut].astype(jnp.float32)
        ).astype(jnp.bfloat16)

    for copy in far_copies + near_copies + x_copies:
        copy.wait_send()
    for n, (b, c, width) in enumerate(chunks):
        others = arrived.at[pl.ds(0, owners - 1), b, :, pl.ds(c, width)]
        pltpu.make_async_copy(others, others, row_send.at[n]).wait()


def write_kernel(*refs):
    count = len(refs) // 2
    sem = refs[-1]
    copies = [pltpu.make_async_copy(refs[n], refs[count + n], sem.at[n]) for n in range(count)]
    for copy in copies:
        copy.start()
    for copy in copies:
        copy.wait()


def fused_body(gradients, master, one, two, synced, rollout, amax, table, shifts):
    owners = lax.axis_size("fsdp")
    rows, cols = master.shape
    blocks = rows // TILE
    part = TILE // owners
    n = len(chunks_of(blocks, cols))
    f32, bf16 = jnp.float32, jnp.bfloat16
    hbm = pl.BlockSpec(memory_space=pltpu.HBM)
    vmem = pl.BlockSpec(memory_space=pltpu.VMEM)
    grouped = (owners, blocks, part, cols)
    whole = (rows, cols)
    dma = pltpu.SemaphoreType.DMA
    results = (
        jax.ShapeDtypeStruct(whole, f32),
        jax.ShapeDtypeStruct(whole, f32),
        jax.ShapeDtypeStruct(whole, f32),
        jax.ShapeDtypeStruct(amax.shape, f32),
        jax.ShapeDtypeStruct(grouped, bf16),
    )
    outs = pl.pallas_call(
        functools.partial(fused_kernel, owners),
        out_shape=tuple(pltpu.VMEM(r.shape, r.dtype) for r in results),
        in_specs=[hbm] * 8 + [pl.BlockSpec(memory_space=pltpu.SMEM)],
        out_specs=(vmem,) * 5,
        scratch_shapes=(
            [pltpu.VMEM(whole, bf16)] * 6
            + [pltpu.VMEM(whole, f32)] * 3
            + [pltpu.VMEM(whole, bf16), pltpu.VMEM(grouped, bf16)]
            + [pltpu.VMEM((blocks, TILE, cols), bf16), pltpu.VMEM(grouped, bf16)]
            + [pltpu.SMEM(amax.shape, f32), pltpu.VMEM((1, TILE), jnp.int32)]
            + [pltpu.VMEM((blocks, cols // TILE, 8, TILE), f32)]
            + [
                dma((9,)), dma((n,)), dma((n,)), dma((blocks,)), dma((blocks,)), dma((n,)), dma((n,)),
                dma((n,)), dma((n,)),
            ]
        ),
        compiler_params=pltpu.CompilerParams(
            collective_id=0, has_side_effects=True, vmem_limit_bytes=32 * 1024 * 1024
        ),
    )(*[
        pltpu.with_memory_space_constraint(x, pltpu.HBM)
        for x in (
            gradients[0], master, one, two, synced, rollout.reshape(grouped), amax,
            table.reshape(1, TILE),
        )
    ], shifts)
    outs = pl.pallas_call(
        write_kernel,
        out_shape=results,
        in_specs=[vmem] * 5,
        out_specs=(hbm,) * 5,
        scratch_shapes=[dma((5,))],
        compiler_params=pltpu.CompilerParams(vmem_limit_bytes=4 * 1024 * 1024),
    )(*[pltpu.with_memory_space_constraint(x, pltpu.VMEM) for x in outs])
    return outs[0], outs[1], outs[2], outs[3], outs[4].reshape(whole)


def owner_rows(row_table, expert_owner, blocks, owner_count):
    per_owner = TILE // owner_count
    ordering = jnp.argsort(row_table, stable=True)
    experts = blocks * TILE // D
    shifts = expert_owner[experts]
    owners = jnp.arange(owner_count, dtype=jnp.int32)
    first_slot = (owners[None, :] - shifts[:, None]) % owner_count * per_owner
    return ordering[first_slot[:, :, None] + jnp.arange(per_owner, dtype=jnp.int32)[None, None, :]]


def plain_body(
    gradients, master, moment_one, moment_two, synced, rollout, amax_record, row_table, expert_owner
):
    owner_count = lax.axis_size("fsdp")
    replica_count = lax.axis_size("dp")
    row_count, column_count = master.shape
    summed = lax.psum_scatter(
        gradients[0].astype(jnp.float32).astype(jnp.bfloat16), "dp", scatter_dimension=1, tiled=True
    ).astype(jnp.float32)
    new_master, new_one, new_two = adam_step(master, moment_one, moment_two, summed / replica_count)
    difference = new_master - synced.astype(jnp.float32)
    block_count = row_count // TILE
    tile_count = column_count // TILE
    tiled_delta = difference.reshape(block_count, TILE, tile_count, TILE)
    new_amax = jnp.max(jnp.abs(tiled_delta), axis=(1, 3))
    scales = amax_record / code_limit
    code_values = (
        jnp.clip(tiled_delta / scales[:, None, :, None], -code_limit, code_limit)
        .astype(jnp.bfloat16)
        .reshape(block_count, TILE, column_count)
    )
    blocks = lax.axis_index("fsdp") * block_count + jnp.arange(block_count, dtype=jnp.int32)
    chosen = owner_rows(row_table, expert_owner, blocks, owner_count)
    per_owner = TILE // owner_count
    ordered = code_values[jnp.arange(block_count, dtype=jnp.int32)[:, None, None], chosen]
    outgoing = jnp.transpose(ordered, (1, 0, 2, 3)).reshape(
        owner_count, block_count * per_owner, column_count
    )
    spread = jnp.broadcast_to(scales[None], (owner_count, block_count, tile_count))
    incoming, scales_in = (
        lax.all_to_all(outgoing, "fsdp", split_axis=0, concat_axis=0, tiled=True),
        lax.all_to_all(
            spread.astype(jnp.bfloat16), "fsdp", split_axis=0, concat_axis=0, tiled=True
        ).astype(spread.dtype),
    )
    restored = (
        incoming.reshape(owner_count, block_count, per_owner, tile_count, TILE).astype(jnp.float32)
        * scales_in[:, :, None, :, None]
    )
    new_rollout = (rollout.astype(jnp.float32) + restored.reshape(row_count, column_count)).astype(
        jnp.bfloat16
    )
    return (new_master, new_one, new_two, new_amax, new_rollout)


def solution(mesh):
    sizes = dict(mesh.shape)
    fits = sizes["dp"] == 4 and sizes["fsdp"] == 8
    return jax.shard_map(
        fused_body if fits else plain_body,
        mesh=mesh,
        in_specs=(
            P("dp", "fsdp", None),
            P("fsdp", "dp"),
            P("fsdp", "dp"),
            P("fsdp", "dp"),
            P("fsdp", "dp"),
            P("fsdp", "dp"),
            P("fsdp", "dp"),
            P(),
            P(),
        ),
        out_specs=(
            P("fsdp", "dp"),
            P("fsdp", "dp"),
            P("fsdp", "dp"),
            P("fsdp", "dp"),
            P("fsdp", "dp"),
        ),
        check_vma=False,
    )
```

```python
import functools

import jax
import jax.numpy as jnp
from jax import lax
from jax.experimental import pallas as pl
from jax.experimental.pallas import tpu as pltpu
from jax.sharding import PartitionSpec as P

D = 7168
TILE = 128
MESH = pl.DeviceIdType.MESH

beta_one = 0.9
beta_two = 0.95
bias_one = 1.0 - 0.9**10
bias_two = 1.0 - 0.95**10
step_size = 0.05
weight_decay = 0.1
adam_floor = 1e-08
code_limit = 448.0


def adam_step(master, moment_one, moment_two, gradient):
    new_one = beta_one * moment_one + (1.0 - beta_one) * gradient
    new_two = beta_two * moment_two + (1.0 - beta_two) * gradient * gradient
    update = new_one / bias_one / (jnp.sqrt(new_two / bias_two) + adam_floor)
    new_master = master - step_size * (update + weight_decay * master)
    return (new_master, new_one, new_two)


SPLIT = 4
WINDOW = 6


def flipped(index, mask):
    out = index
    bit = 1
    while bit <= mask:
        if mask & bit:
            out = out + bit - 2 * bit * (lax.rem(index // bit, 2))
        bit *= 2
    return out


def adam_fast(master, moment_one, moment_two, summed, replicas):
    new_one = beta_one * moment_one + ((1.0 - beta_one) / replicas) * summed
    new_two = beta_two * moment_two + ((1.0 - beta_two) / replicas**2) * (summed * summed)
    root = jnp.sqrt(new_two * (1.0 / bias_two)) + adam_floor
    new_master = (1.0 - step_size * weight_decay) * master - (step_size / bias_one) * new_one / root
    return (new_master, new_one, new_two)


def fused_kernel(
    owners, grads, master, one, two, synced, rollout, amax_h, table_h, shifts,
    master_w, one_w, two_w, amax_out, rollout_w,
    far_own, near_own, far_sib, near_sib, far_sum, far_in,
    master_v, one_v, two_v, synced_v, rollout_v, packed, arrived, amax, table, peaks,
    load_sem, far_send, far_recv, near_send, near_recv, x_send, x_recv, row_send, row_recv,
):
    d = lax.axis_index("dp")
    f = lax.axis_index("fsdp")
    rows, cols = master_v.shape
    blocks = rows // TILE
    width = cols // SPLIT
    part = TILE // owners
    chunks = [(b, h) for b in range(blocks) for h in range(SPLIT)]
    sib = flipped(d, 1)
    opp = flipped(d, 2)
    opp_sib = flipped(d, 3)

    barrier = pltpu.get_barrier_semaphore()
    pl.semaphore_signal(barrier, inc=1, device_id={"dp": sib}, device_id_type=MESH)
    pl.semaphore_signal(barrier, inc=1, device_id={"dp": opp}, device_id_type=MESH)
    for j in range(1, owners):
        pl.semaphore_signal(barrier, inc=1, device_id={"fsdp": flipped(f, j)}, device_id_type=MESH)

    def columns(q):
        return pl.ds(pl.multiple_of(q * cols, cols), cols)

    loads = [
        pltpu.make_async_copy(src, dst, load_sem.at[n])
        for n, (src, dst) in enumerate([
            (table_h, table),
            (amax_h, amax),
            (grads.at[:, columns(opp)], far_own),
            (grads.at[:, columns(d)], near_own),
            (one, one_v),
            (two, two_v),
            (master, master_v),
            (synced, synced_v),
            (rollout, rollout_v),
        ])
    ]
    for load in loads[:4]:
        load.start()

    def chooser(b):
        shift = shifts[((f * blocks + b) * TILE) // D]
        dest = (rank + shift * part) & (TILE - 1)
        return jnp.where(ti == dest, 1.0, 0.0).astype(jnp.bfloat16)

    pl.semaphore_wait(barrier, owners + 1)

    def at(ref, b, h):
        return ref.at[pl.ds(b * TILE, TILE), pl.ds(h * width, width)]

    far_copies = []
    for n, (b, h) in enumerate(chunks):
        source = pl.multiple_of(opp_sib * cols + h * width, width)
        copy = pltpu.make_async_remote_copy(
            src_ref=grads.at[pl.ds(b * TILE, TILE), pl.ds(source, width)],
            dst_ref=at(far_sib, b, h),
            send_sem=far_send.at[n], recv_sem=far_recv.at[n],
            device_id={"dp": sib}, device_id_type=MESH,
        )
        copy.start()
        far_copies.append(copy)
    near_copies = []

    def send_near(b):
        copy = pltpu.make_async_remote_copy(
            src_ref=grads.at[pl.ds(b * TILE, TILE), columns(sib)],
            dst_ref=near_sib.at[pl.ds(b * TILE, TILE), :],
            send_sem=near_send.at[b], recv_sem=near_recv.at[b],
            device_id={"dp": sib}, device_id_type=MESH,
        )
        copy.start()
        near_copies.append(copy)

    send_near(0)
    for load in loads[4:]:
        load.start()

    x_copies = []
    loads[2].wait()

    def send_x(n):
        b, h = chunks[n]
        far_copies[n].wait_recv()
        mine = at(far_own, b, h)[...].astype(jnp.float32)
        theirs = at(far_sib, b, h)[...].astype(jnp.float32)
        at(far_sum, b, h)[...] = (mine + theirs).astype(jnp.bfloat16)
        copy = pltpu.make_async_remote_copy(
            src_ref=at(far_sum, b, h), dst_ref=at(far_in, b, h),
            send_sem=x_send.at[n], recv_sem=x_recv.at[n],
            device_id={"dp": opp}, device_id_type=MESH,
        )
        copy.start()
        x_copies.append(copy)

    for n in range(WINDOW):
        send_x(n)
    for b in range(1, blocks):
        send_near(b)

    for load in loads[:2]:
        load.wait()

    ti = lax.broadcasted_iota(jnp.int32, (TILE, TILE), 0)
    tj = lax.broadcasted_iota(jnp.int32, (TILE, TILE), 1)
    key_row = table[...] * TILE + lax.broadcasted_iota(jnp.int32, (1, TILE), 1)
    key_mat = jnp.broadcast_to(key_row, (TILE, TILE)).astype(jnp.float32)
    key_col = jnp.sum(jnp.where(ti == tj, key_mat, 0.0), axis=1, keepdims=True)
    rank = jnp.sum(jnp.where(key_col < key_mat, 1.0, 0.0), axis=0, keepdims=True).astype(jnp.int32)
    for load in loads[3:]:
        load.wait()

    targets = [flipped(f, j) for j in sorted(range(1, owners), key=lambda j: -(j // 2))]
    choose = None
    for n, (b, h) in enumerate(chunks):
        if h == 0:
            near_copies[b].wait_recv()
            choose = chooser(b)
        if n + WINDOW < len(chunks):
            send_x(n + WINDOW)
        x_copies[n].wait_recv()
        summed = (
            at(near_own, b, h)[...].astype(jnp.float32)
            + at(near_sib, b, h)[...].astype(jnp.float32)
            + at(far_in, b, h)[...].astype(jnp.float32)
        )
        new_master, new_one, new_two = adam_fast(
            at(master_v, b, h)[...], at(one_v, b, h)[...], at(two_v, b, h)[...], summed, 4
        )
        at(master_w, b, h)[...] = new_master
        at(one_w, b, h)[...] = new_one
        at(two_w, b, h)[...] = new_two
        delta = new_master - at(synced_v, b, h)[...].astype(jnp.float32)
        restored = []
        for k in range(width // TILE):
            t = h * (width // TILE) + k
            piece = delta[:, k * TILE : (k + 1) * TILE]
            peaks[b, t] = jnp.max(jnp.abs(piece).reshape(TILE // 8, 8, TILE), axis=0)
            limit = amax[b, t] / code_limit * code_limit
            restored.append(jnp.clip(piece, -limit, limit).astype(jnp.bfloat16))
        restored = jnp.concatenate(restored, axis=1)
        packed[b, :, pl.ds(h * width, width)] = jnp.dot(
            choose, restored, preferred_element_type=jnp.float32
        ).astype(jnp.bfloat16)
        for target in targets:
            pltpu.make_async_remote_copy(
                src_ref=packed.at[b, pl.ds(pl.multiple_of(target * part, part), part), pl.ds(h * width, width)],
                dst_ref=arrived.at[f, b, :, pl.ds(h * width, width)],
                send_sem=row_send.at[n], recv_sem=row_recv.at[n],
                device_id={"fsdp": target}, device_id_type=MESH,
            ).start()
        arrived[f, b, :, pl.ds(h * width, width)] = packed[
            b, pl.ds(pl.multiple_of(f * part, part), part), pl.ds(h * width, width)
        ]

    for b in range(blocks):
        for t in range(cols // TILE):
            top = jnp.max(jnp.max(peaks[b, t], axis=0, keepdims=True), axis=1, keepdims=True)
            amax_out[b : b + 1, t : t + 1] = top

    for n, (b, h) in enumerate(chunks):
        cut = pl.ds(h * width, width)
        others = arrived.at[pl.ds(0, owners - 1), b, :, cut]
        pltpu.make_async_copy(others, others, row_recv.at[n]).wait()
        rollout_w[:, b, :, cut] = (
            rollout_v[:, b, :, cut].astype(jnp.float32) + arrived[:, b, :, cut].astype(jnp.float32)
        ).astype(jnp.bfloat16)

    for copy in far_copies + near_copies + x_copies:
        copy.wait_send()
    for n, (b, h) in enumerate(chunks):
        others = arrived.at[pl.ds(0, owners - 1), b, :, pl.ds(h * width, width)]
        pltpu.make_async_copy(others, others, row_send.at[n]).wait()


def write_kernel(*refs):
    count = len(refs) // 2
    sem = refs[-1]
    copies = [pltpu.make_async_copy(refs[n], refs[count + n], sem.at[n]) for n in range(count)]
    for copy in copies:
        copy.start()
    for copy in copies:
        copy.wait()


def fused_body(gradients, master, one, two, synced, rollout, amax, table, shifts):
    owners = lax.axis_size("fsdp")
    rows, cols = master.shape
    blocks = rows // TILE
    part = TILE // owners
    n = blocks * SPLIT
    f32, bf16 = jnp.float32, jnp.bfloat16
    hbm = pl.BlockSpec(memory_space=pltpu.HBM)
    vmem = pl.BlockSpec(memory_space=pltpu.VMEM)
    grouped = (owners, blocks, part, cols)
    whole = (rows, cols)
    dma = pltpu.SemaphoreType.DMA
    results = (
        jax.ShapeDtypeStruct(whole, f32),
        jax.ShapeDtypeStruct(whole, f32),
        jax.ShapeDtypeStruct(whole, f32),
        jax.ShapeDtypeStruct(amax.shape, f32),
        jax.ShapeDtypeStruct(grouped, bf16),
    )
    outs = pl.pallas_call(
        functools.partial(fused_kernel, owners),
        out_shape=tuple(pltpu.VMEM(r.shape, r.dtype) for r in results),
        in_specs=[hbm] * 8 + [pl.BlockSpec(memory_space=pltpu.SMEM)],
        out_specs=(vmem,) * 5,
        scratch_shapes=(
            [pltpu.VMEM(whole, bf16)] * 6
            + [pltpu.VMEM(whole, f32)] * 3
            + [pltpu.VMEM(whole, bf16), pltpu.VMEM(grouped, bf16)]
            + [pltpu.VMEM((blocks, TILE, cols), bf16), pltpu.VMEM(grouped, bf16)]
            + [pltpu.SMEM(amax.shape, f32), pltpu.VMEM((1, TILE), jnp.int32)]
            + [pltpu.VMEM((blocks, cols // TILE, 8, TILE), f32)]
            + [
                dma((9,)), dma((n,)), dma((n,)), dma((blocks,)), dma((blocks,)), dma((n,)), dma((n,)),
                dma((n,)), dma((n,)),
            ]
        ),
        compiler_params=pltpu.CompilerParams(
            collective_id=0, has_side_effects=True, vmem_limit_bytes=32 * 1024 * 1024
        ),
    )(*[
        pltpu.with_memory_space_constraint(x, pltpu.HBM)
        for x in (
            gradients[0], master, one, two, synced, rollout.reshape(grouped), amax,
            table.reshape(1, TILE),
        )
    ], shifts)
    outs = pl.pallas_call(
        write_kernel,
        out_shape=results,
        in_specs=[vmem] * 5,
        out_specs=(hbm,) * 5,
        scratch_shapes=[dma((5,))],
        compiler_params=pltpu.CompilerParams(vmem_limit_bytes=4 * 1024 * 1024),
    )(*[pltpu.with_memory_space_constraint(x, pltpu.VMEM) for x in outs])
    return outs[0], outs[1], outs[2], outs[3], outs[4].reshape(whole)


def owner_rows(row_table, expert_owner, blocks, owner_count):
    per_owner = TILE // owner_count
    ordering = jnp.argsort(row_table, stable=True)
    experts = blocks * TILE // D
    shifts = expert_owner[experts]
    owners = jnp.arange(owner_count, dtype=jnp.int32)
    first_slot = (owners[None, :] - shifts[:, None]) % owner_count * per_owner
    return ordering[first_slot[:, :, None] + jnp.arange(per_owner, dtype=jnp.int32)[None, None, :]]


def plain_body(
    gradients, master, moment_one, moment_two, synced, rollout, amax_record, row_table, expert_owner
):
    owner_count = lax.axis_size("fsdp")
    replica_count = lax.axis_size("dp")
    row_count, column_count = master.shape
    summed = lax.psum_scatter(
        gradients[0].astype(jnp.float32).astype(jnp.bfloat16), "dp", scatter_dimension=1, tiled=True
    ).astype(jnp.float32)
    new_master, new_one, new_two = adam_step(master, moment_one, moment_two, summed / replica_count)
    difference = new_master - synced.astype(jnp.float32)
    block_count = row_count // TILE
    tile_count = column_count // TILE
    tiled_delta = difference.reshape(block_count, TILE, tile_count, TILE)
    new_amax = jnp.max(jnp.abs(tiled_delta), axis=(1, 3))
    scales = amax_record / code_limit
    code_values = (
        jnp.clip(tiled_delta / scales[:, None, :, None], -code_limit, code_limit)
        .astype(jnp.bfloat16)
        .reshape(block_count, TILE, column_count)
    )
    blocks = lax.axis_index("fsdp") * block_count + jnp.arange(block_count, dtype=jnp.int32)
    chosen = owner_rows(row_table, expert_owner, blocks, owner_count)
    per_owner = TILE // owner_count
    ordered = code_values[jnp.arange(block_count, dtype=jnp.int32)[:, None, None], chosen]
    outgoing = jnp.transpose(ordered, (1, 0, 2, 3)).reshape(
        owner_count, block_count * per_owner, column_count
    )
    spread = jnp.broadcast_to(scales[None], (owner_count, block_count, tile_count))
    incoming, scales_in = (
        lax.all_to_all(outgoing, "fsdp", split_axis=0, concat_axis=0, tiled=True),
        lax.all_to_all(
            spread.astype(jnp.bfloat16), "fsdp", split_axis=0, concat_axis=0, tiled=True
        ).astype(spread.dtype),
    )
    restored = (
        incoming.reshape(owner_count, block_count, per_owner, tile_count, TILE).astype(jnp.float32)
        * scales_in[:, :, None, :, None]
    )
    new_rollout = (rollout.astype(jnp.float32) + restored.reshape(row_count, column_count)).astype(
        jnp.bfloat16
    )
    return (new_master, new_one, new_two, new_amax, new_rollout)


def solution(mesh):
    sizes = dict(mesh.shape)
    fits = sizes["dp"] == 4 and sizes["fsdp"] == 8
    return jax.shard_map(
        fused_body if fits else plain_body,
        mesh=mesh,
        in_specs=(
            P("dp", "fsdp", None),
            P("fsdp", "dp"),
            P("fsdp", "dp"),
            P("fsdp", "dp"),
            P("fsdp", "dp"),
            P("fsdp", "dp"),
            P("fsdp", "dp"),
            P(),
            P(),
        ),
        out_specs=(
            P("fsdp", "dp"),
            P("fsdp", "dp"),
            P("fsdp", "dp"),
            P("fsdp", "dp"),
            P("fsdp", "dp"),
        ),
        check_vma=False,
    )
```

```python
import functools

import jax
import jax.numpy as jnp
from jax import lax
from jax.experimental import pallas as pl
from jax.experimental.pallas import tpu as pltpu
from jax.sharding import PartitionSpec as P

D = 7168
TILE = 128
MESH = pl.DeviceIdType.MESH

beta_one = 0.9
beta_two = 0.95
bias_one = 1.0 - 0.9**10
bias_two = 1.0 - 0.95**10
step_size = 0.05
weight_decay = 0.1
adam_floor = 1e-08
code_limit = 448.0


def adam_step(master, moment_one, moment_two, gradient):
    new_one = beta_one * moment_one + (1.0 - beta_one) * gradient
    new_two = beta_two * moment_two + (1.0 - beta_two) * gradient * gradient
    update = new_one / bias_one / (jnp.sqrt(new_two / bias_two) + adam_floor)
    new_master = master - step_size * (update + weight_decay * master)
    return (new_master, new_one, new_two)


SPLIT = 4
WINDOW = 6


def flipped(index, mask):
    out = index
    bit = 1
    while bit <= mask:
        if mask & bit:
            out = out + bit - 2 * bit * (lax.rem(index // bit, 2))
        bit *= 2
    return out


def adam_fast(master, moment_one, moment_two, summed, replicas):
    new_one = beta_one * moment_one + ((1.0 - beta_one) / replicas) * summed
    new_two = beta_two * moment_two + ((1.0 - beta_two) / replicas**2) * (summed * summed)
    root = jnp.sqrt(new_two * (1.0 / bias_two)) + adam_floor
    new_master = (1.0 - step_size * weight_decay) * master - (step_size / bias_one) * new_one / root
    return (new_master, new_one, new_two)


def fused_kernel(
    owners, grads, master, one, two, synced, rollout, amax_h, table_h, shifts,
    master_w, one_w, two_w, amax_out, rollout_w,
    far_own, near_own, far_sib, near_sib, far_sum, far_in,
    master_v, one_v, two_v, synced_v, rollout_v, packed, arrived, amax, table, peaks,
    load_sem, far_send, far_recv, near_send, near_recv, x_send, x_recv, row_send, row_recv,
):
    d = lax.axis_index("dp")
    f = lax.axis_index("fsdp")
    rows, cols = master_v.shape
    blocks = rows // TILE
    width = cols // SPLIT
    part = TILE // owners
    chunks = [(b, h) for b in range(blocks) for h in range(SPLIT)]
    sib = flipped(d, 1)
    opp = flipped(d, 2)
    opp_sib = flipped(d, 3)

    barrier = pltpu.get_barrier_semaphore()
    pl.semaphore_signal(barrier, inc=1, device_id={"dp": sib}, device_id_type=MESH)
    pl.semaphore_signal(barrier, inc=1, device_id={"dp": opp}, device_id_type=MESH)
    for j in range(1, owners):
        pl.semaphore_signal(barrier, inc=1, device_id={"fsdp": flipped(f, j)}, device_id_type=MESH)

    def columns(q):
        return pl.ds(pl.multiple_of(q * cols, cols), cols)

    loads = [
        pltpu.make_async_copy(src, dst, load_sem.at[n])
        for n, (src, dst) in enumerate([
            (table_h, table),
            (amax_h, amax),
            (grads.at[:, columns(opp)], far_own),
            (grads.at[:, columns(d)], near_own),
            (one, one_v),
            (two, two_v),
            (master, master_v),
            (synced, synced_v),
            (rollout, rollout_v),
        ])
    ]
    for load in loads[:4]:
        load.start()

    def chooser(b):
        shift = shifts[((f * blocks + b) * TILE) // D]
        dest = (rank + shift * part) & (TILE - 1)
        return jnp.where(ti == dest, 1.0, 0.0).astype(jnp.bfloat16)

    pl.semaphore_wait(barrier, owners + 1)

    def at(ref, b, h):
        return ref.at[pl.ds(b * TILE, TILE), pl.ds(h * width, width)]

    far_copies = []
    for n, (b, h) in enumerate(chunks):
        source = pl.multiple_of(opp_sib * cols + h * width, width)
        copy = pltpu.make_async_remote_copy(
            src_ref=grads.at[pl.ds(b * TILE, TILE), pl.ds(source, width)],
            dst_ref=at(far_sib, b, h),
            send_sem=far_send.at[n], recv_sem=far_recv.at[n],
            device_id={"dp": sib}, device_id_type=MESH,
        )
        copy.start()
        far_copies.append(copy)
    near_copies = []

    def send_near(b):
        copy = pltpu.make_async_remote_copy(
            src_ref=grads.at[pl.ds(b * TILE, TILE), columns(sib)],
            dst_ref=near_sib.at[pl.ds(b * TILE, TILE), :],
            send_sem=near_send.at[b], recv_sem=near_recv.at[b],
            device_id={"dp": sib}, device_id_type=MESH,
        )
        copy.start()
        near_copies.append(copy)

    send_near(0)
    for load in loads[4:]:
        load.start()

    x_copies = []
    loads[2].wait()

    def send_x(n):
        b, h = chunks[n]
        far_copies[n].wait_recv()
        mine = at(far_own, b, h)[...].astype(jnp.float32)
        theirs = at(far_sib, b, h)[...].astype(jnp.float32)
        at(far_sum, b, h)[...] = (mine + theirs).astype(jnp.bfloat16)
        copy = pltpu.make_async_remote_copy(
            src_ref=at(far_sum, b, h), dst_ref=at(far_in, b, h),
            send_sem=x_send.at[n], recv_sem=x_recv.at[n],
            device_id={"dp": opp}, device_id_type=MESH,
        )
        copy.start()
        x_copies.append(copy)

    for n in range(WINDOW):
        send_x(n)
    for b in range(1, blocks):
        send_near(b)

    for load in loads[:2]:
        load.wait()

    ti = lax.broadcasted_iota(jnp.int32, (TILE, TILE), 0)
    tj = lax.broadcasted_iota(jnp.int32, (TILE, TILE), 1)
    key_row = table[...] * TILE + lax.broadcasted_iota(jnp.int32, (1, TILE), 1)
    key_mat = jnp.broadcast_to(key_row, (TILE, TILE)).astype(jnp.float32)
    key_col = jnp.sum(jnp.where(ti == tj, key_mat, 0.0), axis=1, keepdims=True)
    rank = jnp.sum(jnp.where(key_col < key_mat, 1.0, 0.0), axis=0, keepdims=True).astype(jnp.int32)
    for load in loads[3:]:
        load.wait()

    targets = [flipped(f, j) for j in sorted(range(1, owners), key=lambda j: -(j // 2))]
    choose = None
    for n, (b, h) in enumerate(chunks):
        if h == 0:
            near_copies[b].wait_recv()
            choose = chooser(b)
        if n + WINDOW < len(chunks):
            send_x(n + WINDOW)
        x_copies[n].wait_recv()
        summed = (
            at(near_own, b, h)[...].astype(jnp.float32)
            + at(near_sib, b, h)[...].astype(jnp.float32)
            + at(far_in, b, h)[...].astype(jnp.float32)
        )
        new_master, new_one, new_two = adam_fast(
            at(master_v, b, h)[...], at(one_v, b, h)[...], at(two_v, b, h)[...], summed, 4
        )
        at(master_w, b, h)[...] = new_master
        at(one_w, b, h)[...] = new_one
        at(two_w, b, h)[...] = new_two
        delta = new_master - at(synced_v, b, h)[...].astype(jnp.float32)
        restored = []
        for k in range(width // TILE):
            t = h * (width // TILE) + k
            piece = delta[:, k * TILE : (k + 1) * TILE]
            peaks[b, t] = jnp.max(jnp.abs(piece).reshape(TILE // 8, 8, TILE), axis=0)
            limit = amax[b, t] / code_limit * code_limit
            restored.append(jnp.clip(piece, -limit, limit).astype(jnp.bfloat16))
        restored = jnp.concatenate(restored, axis=1)
        packed[b, :, pl.ds(h * width, width)] = jnp.dot(
            choose, restored, preferred_element_type=jnp.float32
        ).astype(jnp.bfloat16)
        for target in targets[:: 1 - 2 * (n % 2)]:
            pltpu.make_async_remote_copy(
                src_ref=packed.at[b, pl.ds(pl.multiple_of(target * part, part), part), pl.ds(h * width, width)],
                dst_ref=arrived.at[f, b, :, pl.ds(h * width, width)],
                send_sem=row_send.at[n], recv_sem=row_recv.at[n],
                device_id={"fsdp": target}, device_id_type=MESH,
            ).start()
        arrived[f, b, :, pl.ds(h * width, width)] = packed[
            b, pl.ds(pl.multiple_of(f * part, part), part), pl.ds(h * width, width)
        ]

    for b in range(blocks):
        for t in range(cols // TILE):
            top = jnp.max(jnp.max(peaks[b, t], axis=0, keepdims=True), axis=1, keepdims=True)
            amax_out[b : b + 1, t : t + 1] = top

    for n, (b, h) in enumerate(chunks):
        cut = pl.ds(h * width, width)
        others = arrived.at[pl.ds(0, owners - 1), b, :, cut]
        pltpu.make_async_copy(others, others, row_recv.at[n]).wait()
        rollout_w[:, b, :, cut] = (
            rollout_v[:, b, :, cut].astype(jnp.float32) + arrived[:, b, :, cut].astype(jnp.float32)
        ).astype(jnp.bfloat16)

    for copy in far_copies + near_copies + x_copies:
        copy.wait_send()
    for n, (b, h) in enumerate(chunks):
        others = arrived.at[pl.ds(0, owners - 1), b, :, pl.ds(h * width, width)]
        pltpu.make_async_copy(others, others, row_send.at[n]).wait()


def write_kernel(*refs):
    count = len(refs) // 2
    sem = refs[-1]
    copies = [pltpu.make_async_copy(refs[n], refs[count + n], sem.at[n]) for n in range(count)]
    for copy in copies:
        copy.start()
    for copy in copies:
        copy.wait()


def fused_body(gradients, master, one, two, synced, rollout, amax, table, shifts):
    owners = lax.axis_size("fsdp")
    rows, cols = master.shape
    blocks = rows // TILE
    part = TILE // owners
    n = blocks * SPLIT
    f32, bf16 = jnp.float32, jnp.bfloat16
    hbm = pl.BlockSpec(memory_space=pltpu.HBM)
    vmem = pl.BlockSpec(memory_space=pltpu.VMEM)
    grouped = (owners, blocks, part, cols)
    whole = (rows, cols)
    dma = pltpu.SemaphoreType.DMA
    results = (
        jax.ShapeDtypeStruct(whole, f32),
        jax.ShapeDtypeStruct(whole, f32),
        jax.ShapeDtypeStruct(whole, f32),
        jax.ShapeDtypeStruct(amax.shape, f32),
        jax.ShapeDtypeStruct(grouped, bf16),
    )
    outs = pl.pallas_call(
        functools.partial(fused_kernel, owners),
        out_shape=tuple(pltpu.VMEM(r.shape, r.dtype) for r in results),
        in_specs=[hbm] * 8 + [pl.BlockSpec(memory_space=pltpu.SMEM)],
        out_specs=(vmem,) * 5,
        scratch_shapes=(
            [pltpu.VMEM(whole, bf16)] * 6
            + [pltpu.VMEM(whole, f32)] * 3
            + [pltpu.VMEM(whole, bf16), pltpu.VMEM(grouped, bf16)]
            + [pltpu.VMEM((blocks, TILE, cols), bf16), pltpu.VMEM(grouped, bf16)]
            + [pltpu.SMEM(amax.shape, f32), pltpu.VMEM((1, TILE), jnp.int32)]
            + [pltpu.VMEM((blocks, cols // TILE, 8, TILE), f32)]
            + [
                dma((9,)), dma((n,)), dma((n,)), dma((blocks,)), dma((blocks,)), dma((n,)), dma((n,)),
                dma((n,)), dma((n,)),
            ]
        ),
        compiler_params=pltpu.CompilerParams(
            collective_id=0, has_side_effects=True, vmem_limit_bytes=32 * 1024 * 1024
        ),
    )(*[
        pltpu.with_memory_space_constraint(x, pltpu.HBM)
        for x in (
            gradients[0], master, one, two, synced, rollout.reshape(grouped), amax,
            table.reshape(1, TILE),
        )
    ], shifts)
    outs = pl.pallas_call(
        write_kernel,
        out_shape=results,
        in_specs=[vmem] * 5,
        out_specs=(hbm,) * 5,
        scratch_shapes=[dma((5,))],
        compiler_params=pltpu.CompilerParams(vmem_limit_bytes=4 * 1024 * 1024),
    )(*[pltpu.with_memory_space_constraint(x, pltpu.VMEM) for x in outs])
    return outs[0], outs[1], outs[2], outs[3], outs[4].reshape(whole)


def owner_rows(row_table, expert_owner, blocks, owner_count):
    per_owner = TILE // owner_count
    ordering = jnp.argsort(row_table, stable=True)
    experts = blocks * TILE // D
    shifts = expert_owner[experts]
    owners = jnp.arange(owner_count, dtype=jnp.int32)
    first_slot = (owners[None, :] - shifts[:, None]) % owner_count * per_owner
    return ordering[first_slot[:, :, None] + jnp.arange(per_owner, dtype=jnp.int32)[None, None, :]]


def plain_body(
    gradients, master, moment_one, moment_two, synced, rollout, amax_record, row_table, expert_owner
):
    owner_count = lax.axis_size("fsdp")
    replica_count = lax.axis_size("dp")
    row_count, column_count = master.shape
    summed = lax.psum_scatter(
        gradients[0].astype(jnp.float32).astype(jnp.bfloat16), "dp", scatter_dimension=1, tiled=True
    ).astype(jnp.float32)
    new_master, new_one, new_two = adam_step(master, moment_one, moment_two, summed / replica_count)
    difference = new_master - synced.astype(jnp.float32)
    block_count = row_count // TILE
    tile_count = column_count // TILE
    tiled_delta = difference.reshape(block_count, TILE, tile_count, TILE)
    new_amax = jnp.max(jnp.abs(tiled_delta), axis=(1, 3))
    scales = amax_record / code_limit
    code_values = (
        jnp.clip(tiled_delta / scales[:, None, :, None], -code_limit, code_limit)
        .astype(jnp.bfloat16)
        .reshape(block_count, TILE, column_count)
    )
    blocks = lax.axis_index("fsdp") * block_count + jnp.arange(block_count, dtype=jnp.int32)
    chosen = owner_rows(row_table, expert_owner, blocks, owner_count)
    per_owner = TILE // owner_count
    ordered = code_values[jnp.arange(block_count, dtype=jnp.int32)[:, None, None], chosen]
    outgoing = jnp.transpose(ordered, (1, 0, 2, 3)).reshape(
        owner_count, block_count * per_owner, column_count
    )
    spread = jnp.broadcast_to(scales[None], (owner_count, block_count, tile_count))
    incoming, scales_in = (
        lax.all_to_all(outgoing, "fsdp", split_axis=0, concat_axis=0, tiled=True),
        lax.all_to_all(
            spread.astype(jnp.bfloat16), "fsdp", split_axis=0, concat_axis=0, tiled=True
        ).astype(spread.dtype),
    )
    restored = (
        incoming.reshape(owner_count, block_count, per_owner, tile_count, TILE).astype(jnp.float32)
        * scales_in[:, :, None, :, None]
    )
    new_rollout = (rollout.astype(jnp.float32) + restored.reshape(row_count, column_count)).astype(
        jnp.bfloat16
    )
    return (new_master, new_one, new_two, new_amax, new_rollout)


def solution(mesh):
    sizes = dict(mesh.shape)
    fits = sizes["dp"] == 4 and sizes["fsdp"] == 8
    return jax.shard_map(
        fused_body if fits else plain_body,
        mesh=mesh,
        in_specs=(
            P("dp", "fsdp", None),
            P("fsdp", "dp"),
            P("fsdp", "dp"),
            P("fsdp", "dp"),
            P("fsdp", "dp"),
            P("fsdp", "dp"),
            P("fsdp", "dp"),
            P(),
            P(),
        ),
        out_specs=(
            P("fsdp", "dp"),
            P("fsdp", "dp"),
            P("fsdp", "dp"),
            P("fsdp", "dp"),
            P("fsdp", "dp"),
        ),
        check_vma=False,
    )
```
